128 devices in a mesh: member: 4 (over x_lo, core), space: 32 (over y, z, x_hi).
Axes of the slice: x: 4 (x_hi: 2, x_lo: 2; x = x_hi * 2 + x_lo), y: 4, z: 4, core: 2. Of those that a mesh axis runs over, the one named last changes fastest.
Arguments:
- latent: bfloat16 [16, 512, 1024], P('member', 'space'), may hold values from -6 to 6
- edge_index: int32 [3, 4096], P(None, 'space'), may hold values from 0 to 23, as said below
- edge_weight: float32 [3, 4096], P(None, 'space'), may hold values from 0.25 to 1
- noise_seed: int32 [16], P('member'), may hold values from 0 to 63
- noise_table: float32 [64, 1024], replicated, may hold values from -1.5 to 1.5
- w_in: bfloat16 [1024, 4096], P('space'), may hold values from -0.1875 to 0.1875
- w_out: bfloat16 [100, 4096], replicated, may hold values from -0.09375 to 0.09375
- target: float32 [100, 4096], P(None, 'space'), may hold values from -5 to 5
- area_weight: float32 [4096], P('space'), may hold values from 1 to 30, as said below
Outputs:
- loss: float32 [], replicated
- grad_latent: float32 [16, 512, 1024], P('member', 'space')
- grad_w_in: float32 [1024, 4096], P('space')
- grad_w_out: float32 [100, 4096], replicated
The draws below stay inside these ranges and needn't reach their ends.
Inputs may be any that keep to these rules, and one draw needn't show every extreme that they name: `edge_index`: entry [k, p] indexes the extended block of the shard that holds point p: rows below 4 are the last 4 nodes of the previous shard, the next 16 rows its own nodes, the last 4 rows the first nodes of the next shard. Every edge lies within 4 nodes of the point's own node. `area_weight`: Positive.
All inputs are finite; a program needn't handle non-finite values.
Results may differ from the reference program's by a relative error of at most 0.0036.
The reference program's roundings to bfloat16 on the way (of `window`, `normed`, `hidden`, `grad_fields` and `grad_pre`) count: a program that leaves them out, or rounds other values in their place, can miss the bound.
Values may be sent and summed in bfloat16 or wider, within the bound.
A program may use at most 128 MiB of HBM per device.

```python
import math
from functools import partial
import jax
import jax.numpy as jnp
from jax import lax

LAT = 1024
VARS = 100
HID = 4096
PTS_DEV = 128
K = 3
NOISE_TAB = 64
NODE_DEV = 16
HALO = 4
MEMBERS = 16
POINTS = 4096
NODES = 512
N_SPACE = 32


def draw_edge_index(key, part):
    key = jax.random.fold_in(key, 11)
    ext_rows = NODE_DEV + 2 * HALO
    point_ids = jnp.arange(POINTS, dtype=jnp.int32)
    local_ids = point_ids % PTS_DEV
    centre_rows = HALO + local_ids * NODE_DEV // PTS_DEV
    offsets = jax.random.randint(key, (K, POINTS), -HALO, HALO + 1, dtype=jnp.int32)
    indices = jnp.clip(centre_rows[None, :] + offsets, 0, ext_rows - 1)
    first_row = jnp.where(local_ids == 0, 0, jnp.where(local_ids == PTS_DEV - 1, ext_rows - 1, indices[0]))
    indices = indices.at[0].set(first_row)
    return indices.astype(jnp.int32)


def draw_area_weight(key, part):
    key = jax.random.fold_in(key, 17)
    positions = jnp.arange(POINTS, dtype=jnp.float32)
    ramp_part = jnp.exp(math.log(3.0) * positions / POINTS)
    factor = jnp.exp(jax.random.uniform(key, (POINTS,), jnp.float32, 0.0, math.log(4.0)))
    return (ramp_part * factor).astype(jnp.float32)


def touch_ends(entries, stream_key, least, largest):
    place = [jax.random.randint(jax.random.fold_in(stream_key, axis), (), 0, length) for axis, length in enumerate(entries.shape)]
    main_axis = entries.shape.index(max(entries.shape))
    neighbour = place[:main_axis] + [(place[main_axis] + 1) % entries.shape[main_axis]] + place[main_axis + 1:]
    return entries.at[tuple(place)].set(least).at[tuple(neighbour)].set(largest)


def level_of(rng, dims, cuts, low, largest):
    factor_of, own = 1.0, jax.random.fold_in(rng, 6)
    for position, shards_of in cuts:
        steps = jnp.exp(jax.random.uniform(jax.random.fold_in(own, position), (shards_of,), jnp.float32, low / len(cuts), largest / len(cuts)))
        factor_of = factor_of * jnp.repeat(steps, dims[position] // shards_of).reshape([-1 if axis == position else 1 for axis in range(len(dims))])
    return factor_of


def noise(rng, shape, width, bound, cuts=(), kind=jnp.bfloat16):
    array = jax.random.normal(rng, shape, jnp.float32) * width
    if len(cuts) > 0:
        array = level_of(rng, shape, cuts, -0.22, 0.18) * array
    return jnp.clip(array, min=-bound, max=bound).astype(kind)


def setup_inputs(seed: int = 0) -> dict:
    arg_keys = jax.random.split(jax.random.key(seed), 10)
    latent = noise(arg_keys[0], (MEMBERS, NODES, LAT), 1.0, 6.0, ((0, 4), (1, 32)))
    edge_index = draw_edge_index(jax.random.fold_in(arg_keys[9], 71), 0)
    edge_weight = jnp.clip(jnp.exp(math.log(1.0) - 1.3862944 * jax.random.uniform(arg_keys[2], (K, POINTS), jnp.float32) ** level_of(arg_keys[2], (K, POINTS), ((1, 32),), -0.2, 0.2)), 0.25, 1.0)
    noise_seed = touch_ends(jax.random.randint(arg_keys[3], (MEMBERS,), 0, NOISE_TAB), jax.random.fold_in(arg_keys[3], 1), 0, NOISE_TAB - 1).astype(jnp.int32)
    noise_table = noise(arg_keys[4], (NOISE_TAB, LAT), 0.3, 1.5, (), jnp.float32)
    w_in = noise(arg_keys[5], (LAT, HID), LAT ** -0.5, 0.1875, ((0, 32),))
    w_out = noise(arg_keys[6], (VARS, HID), HID ** -0.5, 0.09375)
    target = noise(arg_keys[7], (VARS, POINTS), 0.7, 5.0, ((1, 32),), jnp.float32)
    area_weight = draw_area_weight(jax.random.fold_in(arg_keys[9], 71), 0)
    return dict(latent=latent, edge_index=edge_index, edge_weight=edge_weight, noise_seed=noise_seed, noise_table=noise_table, w_in=w_in, w_out=w_out, target=target, area_weight=area_weight)


epsilon = 1e-05
smoothing_sq = 0.04
loss_scale = 1024.0

def normalize(aggregate, member_scale):
    average = lax.optimization_barrier(jnp.mean(aggregate, axis=-1, keepdims=True))
    centred = aggregate - average
    spread = lax.optimization_barrier(jnp.mean(centred * centred, axis=-1, keepdims=True))
    return centred * lax.rsqrt(spread + epsilon) * member_scale[:, None, :]

def smooth_abs(difference):
    return jnp.sqrt(difference * difference + smoothing_sq)

def smooth_slope(difference):
    return difference * lax.rsqrt(difference * difference + smoothing_sq)

def build_table(edge_index, edge_weight, ext_rows):
    node_ids = lax.broadcasted_iota(jnp.int32, (1, 1, ext_rows), 2)
    matches = jnp.where(edge_index[:, :, None] == node_ids, edge_weight[:, :, None], jnp.zeros((), edge_weight.dtype))
    return lax.optimization_barrier(jnp.sum(matches, axis=0))

def reference(latent, edge_index, edge_weight, noise_seed, noise_table, w_in, w_out, target, area_weight):
    highest = lax.Precision.HIGHEST
    members = MEMBERS
    ext_rows = NODE_DEV + 2 * HALO
    padded = jnp.pad(latent, ((0, 0), (HALO, HALO), (0, 0)))
    member_scale = 1.0 + noise_table[noise_seed]
    pair_norm = 1.0 / (members * (members - 1))
    w_in32 = w_in.astype(jnp.float32)
    w_out32 = w_out.astype(jnp.float32)

    def shard_step(totals, shard_index):
        grad_in, grad_out, loss_sum, grad_pad = totals
        node_start = (shard_index * NODE_DEV).astype(jnp.int32)
        point_start = (shard_index * PTS_DEV).astype(jnp.int32)
        window = lax.dynamic_slice_in_dim(padded, node_start, ext_rows, 1).astype(jnp.float32)
        index_block = lax.dynamic_slice_in_dim(edge_index, point_start, PTS_DEV, 1)
        weight_block = lax.dynamic_slice_in_dim(edge_weight, point_start, PTS_DEV, 1)
        weights_table = build_table(index_block, weight_block, ext_rows)
        aggregate = jnp.einsum('pe,med->mpd', weights_table, window, precision=highest)
        normed = normalize(aggregate, member_scale).astype(jnp.bfloat16)
        pre_act = jnp.einsum('mpd,dh->mph', normed.astype(jnp.float32), w_in32, precision=highest)
        hidden = jax.nn.gelu(pre_act).astype(jnp.bfloat16)
        fields = jnp.einsum('mph,vh->mvp', hidden.astype(jnp.float32), w_out32, precision=highest)
        local_target = lax.dynamic_slice_in_dim(target, point_start, PTS_DEV, 1)
        local_area = lax.dynamic_slice_in_dim(area_weight, point_start, PTS_DEV, 0)
        abs_pairs = jnp.zeros_like(fields)
        sign_pairs = jnp.zeros_like(fields)
        for member_row in range(members):
            difference = fields - fields[member_row][None]
            abs_pairs = abs_pairs + smooth_abs(difference)
            sign_pairs = sign_pairs + smooth_slope(difference)
        misfit = fields - local_target[None]
        weighted = local_area[None, None, :] / VARS
        loss_term = jnp.sum(weighted * (smooth_abs(misfit) / members - 0.5 * pair_norm * abs_pairs))
        grad_fields = (loss_scale * weighted * (smooth_slope(misfit) / members - pair_norm * sign_pairs)).astype(jnp.bfloat16)
        grad_fields32 = grad_fields.astype(jnp.float32)
        grad_out_part = jnp.einsum('mph,mvp->vh', hidden.astype(jnp.float32), grad_fields32, precision=highest)
        grad_hidden = jnp.einsum('mvp,vh->mph', grad_fields32, w_out32, precision=highest)
        unused, gelu_back = jax.vjp(jax.nn.gelu, pre_act)
        grad_pre = gelu_back(grad_hidden)[0].astype(jnp.bfloat16)
        grad_in_part = jnp.einsum('mpd,mph->dh', normed.astype(jnp.float32), grad_pre.astype(jnp.float32), precision=highest)
        grad_normed = jnp.einsum('mph,dh->mpd', grad_pre.astype(jnp.float32), w_in32, precision=highest)
        unused2, norm_back = jax.vjp(partial(normalize, member_scale=member_scale), aggregate)
        grad_aggregate = norm_back(grad_normed)[0]
        grad_window = jnp.einsum('pe,mpd->med', weights_table, grad_aggregate, precision=highest)
        current = lax.dynamic_slice_in_dim(grad_pad, node_start, ext_rows, 1)
        grad_pad = lax.dynamic_update_slice_in_dim(grad_pad, current + grad_window, node_start, 1)
        return ((grad_in + grad_in_part, grad_out + grad_out_part, loss_sum + loss_term, grad_pad), None)
    start_totals = (jnp.zeros((LAT, HID), jnp.float32), jnp.zeros((VARS, HID), jnp.float32), jnp.zeros((), jnp.float32), jnp.zeros((members, NODES + 2 * HALO, LAT), jnp.float32))
    totals, unused3 = lax.scan(shard_step, start_totals, jnp.arange(N_SPACE, dtype=jnp.int32))
    grad_in, grad_out, loss_sum, grad_pad = totals
    return (loss_sum / POINTS, grad_pad[:, HALO:HALO + NODES], grad_in / loss_scale, grad_out / loss_scale)
```

```python
import jax
import jax.numpy as jnp
from jax import lax
from jax.experimental import pallas as pl
from jax.experimental.pallas import tpu as pltpu
from jax.sharding import PartitionSpec as P

VARS = 100
HALO = 4
MEMBERS = 16
POINTS = 4096
F32 = jnp.float32
BF16 = jnp.bfloat16
EPS = 1e-05
SMOOTH = 0.04
SCALE = 1024.0
PAIR = 1.0 / (MEMBERS * (MEMBERS - 1))
GELU_C = 0.7978845608028654
MESH = pl.DeviceIdType.MESH

LAT = 1024
HALF = 2048
WIDE = HALF + 256
PARTS = [(0, 384), (384, 384), (768, 384), (1152, 384), (1536, 256), (1792, 256)]
ORDERS = ["yzx", "zxy", "xyz", "yxz", "zyx", "xzy"]
OUT_PARTS = [(2048, 128), (2176, 128)]
OUT_ORDERS = ["zyx", "xzy"]
ALL_PARTS = PARTS + OUT_PARTS
ALL_ORDERS = ORDERS + OUT_ORDERS

DMA = pltpu.SemaphoreType.DMA
SCRATCH = dict(
    wbuf=pltpu.VMEM((4, 4, 4, 16, HALF), BF16),
    wo=pltpu.VMEM((128, HALF), BF16),
    nbuf=pltpu.VMEM((8, 128, LAT), BF16),
    n_t=pltpu.VMEM((LAT, 1024), BF16),
    xhat=pltpu.VMEM((4, 128, LAT), F32),
    rstd=pltpu.VMEM((4, 128, 128), F32),
    tab=pltpu.VMEM((128, 128), F32),
    small=pltpu.VMEM((3, 128, 128), F32),
    hid=pltpu.VMEM((1024, HALF), BF16),
    big=pltpu.VMEM((4, 4, 4, 16, WIDE), F32),
    gpre=pltpu.VMEM((1024, HALF), BF16),
    halo_s=pltpu.VMEM((2, 16, LAT), BF16),
    halo_r=pltpu.VMEM((2, 16, LAT), BF16),
    fpart=pltpu.VMEM((8, 4, 32, 128), F32),
    fcore=pltpu.VMEM((8, 2, 32, 128), F32),
    fsum=pltpu.VMEM((2, 8, 32, 128), F32),
    fother=pltpu.VMEM((8, 32, 128), F32),
    gf=pltpu.VMEM((8, 4, 32, 128), BF16),
    gfo=pltpu.VMEM((8, 32, 128), BF16),
    gf_t=pltpu.VMEM((128, 1024), BF16),
    sb1=pltpu.VMEM((4, 4, 4, 16, WIDE), BF16),
    rb1=pltpu.VMEM((3, 4, 4, 16, WIDE), BF16),
    q1=pltpu.VMEM((4, 4, 16, WIDE), F32),
    sb2=pltpu.VMEM((4, 4, 16, WIDE), BF16),
    rb2=pltpu.VMEM((3, 4, 16, WIDE), BF16),
    q2=pltpu.VMEM((4, 16, WIDE), F32),
    sb3=pltpu.VMEM((4, 16, WIDE), BF16),
    rb3=pltpu.VMEM((3, 16, WIDE), BF16),
    fin=pltpu.VMEM((2, 2, 16, HALF), F32),
    obuf=pltpu.VMEM((2, 4, 4, 4, 16, 256), BF16),
    gno=pltpu.VMEM((4, 128, LAT), F32),
    gns=pltpu.VMEM((4, 128, LAT), BF16),
    gnr=pltpu.VMEM((4, 128, LAT), BF16),
    rim_s=pltpu.VMEM((2, 16, LAT), F32),
    rim_r=pltpu.VMEM((2, 16, LAT), F32),
    loss_s=pltpu.VMEM((4, 8, 128), F32),
    loss_r=pltpu.VMEM((10, 8, 128), F32),
    ag_ss=DMA((6, 3, 3)),
    ag_rs=DMA((6, 3, 3)),
    rs_ss=DMA((8, 3, 3)),
    rs_rs=DMA((8, 3, 3)),
    oa_ss=DMA((2, 3, 3)),
    oa_rs=DMA((2, 3, 3)),
    fin_ss=DMA((6, 3)),
    fin_rs=DMA((6, 3)),
    n_ss=DMA((4,)),
    n_rs=DMA((4,)),
    gn_ss=DMA((4,)),
    gn_rs=DMA((4,)),
    halo_ss=DMA((2,)),
    halo_rs=DMA((2,)),
    rim_ss=DMA((2,)),
    rim_rs=DMA((2,)),
    f_ss=DMA((2,)),
    f_rs=DMA((2,)),
    g_ss=DMA((3,)),
    g_rs=DMA((3,)),
    oc_ss=DMA,
    oc_rs=DMA,
    l_ss=DMA((10,)),
    l_rs=DMA((10,)),
)


def dot(a, b, dims=((1,), (0,)), precision=None):
    return lax.dot_general(a, b, (dims, ((), ())), precision=precision, preferred_element_type=F32)


class Place:
    def __init__(self):
        m, s = lax.axis_index("member"), lax.axis_index("space")
        self.m, self.s = m, s
        self.xl, self.core = m // 2, m % 2
        self.y, self.z, self.xh = s // 8, (s // 2) % 4, s % 2
        self.x = self.xh * 2 + self.xl

    def device(self, y, z, x):
        return ((x % 2) * 2 + self.core, (y * 4 + z) * 2 + x // 2)

    def at(self, axis):
        return getattr(self, axis)

    def peer(self, axis, step):
        q = dict(y=self.y, z=self.z, x=self.x)
        q[axis] = (q[axis] + step) % 4
        return self.device(**q)

    def core_peer(self):
        return (self.xl * 2 + 1 - self.core, self.s)

    def pair_peer(self):
        return ((1 - self.xl) * 2 + self.core, self.s)

    def cross_peer(self):
        return ((1 - self.xl) * 2 + 1 - self.core, self.s)

    def shard(self, step):
        return (self.m, (self.s + step + 32) % 32)


class Copies:
    def __init__(self):
        self.sent = []

    def send(self, src, dst, ss, rs, device):
        copy = pltpu.make_async_remote_copy(
            src_ref=src, dst_ref=dst, send_sem=ss, recv_sem=rs, device_id=device, device_id_type=MESH
        )
        copy.start()
        self.sent.append(copy)
        return copy

    def drain(self):
        for copy in self.sent:
            copy.wait_send()


def arrive(copies):
    for copy in copies:
        copy.wait_recv()


def kernel(lat, eidx, ewt, seed, ntab, w_in, w_out, target, area, loss_o, gl_o, gwi_o, gwo_o, *refs):
    r = dict(zip(SCRATCH, refs))
    wbuf, big, nbuf, n_t, hid, gpre, wo = (r[k] for k in ("wbuf", "big", "nbuf", "n_t", "hid", "gpre", "wo"))
    xhat, rstd, tab, small = r["xhat"], r["rstd"], r["tab"], r["small"]
    me = Place()
    c = Copies()
    col0 = pl.multiple_of(me.core * HALF, 128)

    friends = [me.peer(a, k) for a in "yzx" for k in (1, 2, 3)]
    friends += [me.core_peer(), me.cross_peer(), me.shard(1), me.shard(-1)]
    barrier = pltpu.get_barrier_semaphore()
    for d in friends:
        pl.semaphore_signal(barrier, inc=1, device_id=d, device_id_type=MESH)

    wbuf[me.y, me.z, me.x] = w_in[pl.ds(pl.multiple_of(me.xl * 16, 16), 16), pl.ds(col0, HALF)]
    lat32 = [lat[i].astype(F32) for i in range(4)]
    r["halo_s"][0] = jnp.concatenate([v[12:16] for v in lat32], axis=0).astype(BF16)
    r["halo_s"][1] = jnp.concatenate([v[0:4] for v in lat32], axis=0).astype(BF16)
    pl.semaphore_wait(barrier, len(friends))

    halo = [
        c.send(r["halo_s"].at[0], r["halo_r"].at[0], r["halo_ss"].at[0], r["halo_rs"].at[0], me.shard(1)),
        c.send(r["halo_s"].at[1], r["halo_r"].at[1], r["halo_ss"].at[1], r["halo_rs"].at[1], me.shard(-1)),
    ]

    gathered = {}

    def gather_stage(stage):
        for k, (c0, cw) in enumerate(PARTS):
            arrive(gathered.get(k, []))
            order = ORDERS[k]
            index = tuple(pl.ds(0, 4) if a in order[:stage] else pl.ds(me.at(a), 1) for a in "yzx")
            index += (slice(None), pl.ds(c0, cw))
            gathered[k] = [
                c.send(
                    wbuf.at[index], wbuf.at[index], r["ag_ss"].at[k, stage, i - 1], r["ag_rs"].at[k, stage, i - 1],
                    me.peer(order[stage], i),
                )
                for i in (2, 1, 3)
            ]

    gather_stage(0)

    node = lax.broadcasted_iota(jnp.int32, (128, 128), 0)
    row_of = jnp.where(node < 16, node + HALO, jnp.where(node < 20, node - 16, jnp.where(node < 24, node, -1)))
    table_t = jnp.zeros((128, 128), F32)
    for k in range(3):
        table_t = table_t + jnp.where(row_of == eidx[k : k + 1, :], ewt[k : k + 1, :], 0.0)
    tab[...] = table_t
    table = table_t.T[:, :32]
    t_hi = table.astype(BF16)
    t_rest = table - t_hi.astype(F32)
    t_mid = t_rest.astype(BF16)
    t_low = (t_rest - t_mid.astype(F32)).astype(BF16)
    small[0] = jnp.zeros((128, 128), F32)
    small[0, 0:VARS] = target[...]
    small[1] = small[0].T
    small[2] = jnp.broadcast_to(area[...], (128, 128)).T

    arrive(halo)
    has_prev = (me.s > 0).astype(F32)
    has_next = (me.s < 31).astype(F32)
    normed = []
    for i in range(4):
        prev = r["halo_r"][0].astype(F32)[4 * i : 4 * i + 4] * has_prev
        nxt = r["halo_r"][1].astype(F32)[4 * i : 4 * i + 4] * has_next
        window = jnp.concatenate([lat[i].astype(F32), prev, nxt, jnp.zeros((8, LAT), F32)], axis=0).astype(BF16)
        xhat[i] = dot(t_hi, window) + dot(t_mid, window) + dot(t_low, window)
        scale = 1.0 + ntab[pl.ds(seed[i], 1), :]
        row = me.core * 4 + i

        @pl.loop(0, 4)
        def _(j):
            rows = pl.ds(pl.multiple_of(j * 32, 32), 32)
            a = xhat[i, rows, :]
            centred = a - jnp.mean(a, axis=-1, keepdims=True)
            inv = lax.rsqrt(jnp.mean(centred * centred, axis=-1, keepdims=True) + EPS)
            unit = centred * inv
            xhat[i, rows, :] = unit
            rstd[i, rows, :] = jnp.broadcast_to(inv, (32, 128))
            nbuf[row, rows, :] = (unit * scale).astype(BF16)

        normed.append(c.send(nbuf.at[row], nbuf.at[row], r["n_ss"].at[i], r["n_rs"].at[i], me.core_peer()))
        if i == 1:
            gather_stage(1)

    big[0, 0:2, :, :, 0:HALF] = jnp.zeros((2, 4, 16, HALF), F32)
    head = w_out[:, pl.ds(col0, HALF)].astype(F32)
    for v in range(6):
        big[0, v // 4, v % 4, :, 0:HALF] = head[16 * v : 16 * v + 16]
    big[0, 1, 2, 0:4, 0:HALF] = head[96:100]
    wo[...] = big[0, 0:2, :, :, 0:HALF].reshape(128, HALF).astype(BF16)

    gather_stage(2)
    arrive(normed)
    for i in range(8):
        n_t[:, 128 * i : 128 * i + 128] = nbuf[i].T
    for k in range(6):
        arrive(gathered[k])

    @pl.loop(0, HALF // 256)
    def _(j):
        cols = pl.ds(pl.multiple_of(j * 256, 256), 256)
        w = wbuf[:, :, :, :, cols].reshape(LAT, 256)
        for h in range(4):
            pre = dot(nbuf[2 * h : 2 * h + 2].reshape(256, LAT), w)
            sq = pre * pre
            t = jnp.tanh(pre * (GELU_C + (GELU_C * 0.044715) * sq))
            cdf = 0.5 + 0.5 * t
            hid[256 * h : 256 * h + 256, cols] = (pre * cdf).astype(BF16)
            slope = cdf + (0.5 * pre) * (1.0 - t * t) * (GELU_C + (3.0 * GELU_C * 0.044715) * sq)
            big[h, :, :, :, cols] = slope.reshape(4, 4, 16, 256)

    for h in range(4):
        part = dot(hid[256 * h : 256 * h + 256, :], wo[...], ((1,), (1,)))
        r["fpart"][2 * h : 2 * h + 2] = part.reshape(2, 4, 32, 128)

    fpart, fcore, fsum, fother, gf, gfo = (r[k] for k in ("fpart", "fcore", "fsum", "fother", "gf", "gfo"))
    f1 = c.send(
        fpart.at[:, pl.ds(2 * (1 - me.core), 2)], fcore, r["f_ss"].at[0], r["f_rs"].at[0], me.core_peer()
    )
    f1.wait_recv()
    for g in range(2):
        fsum[g] = fpart[:, 2 * me.core + g] + fcore[:, g]
    f2 = c.send(fsum.at[1 - me.xl], fother, r["f_ss"].at[1], r["f_rs"].at[1], me.pair_peer())
    group = me.core * 2 + me.xl
    f2.wait_recv()

    r["loss_s"][0] = jnp.zeros((8, 128), F32)
    lane = lax.broadcasted_iota(jnp.int32, (8, 128), 1)

    @pl.loop(0, 4)
    def _(j):
        rows = pl.ds(pl.multiple_of(j * 8, 8), 8)
        point = pl.ds(pl.multiple_of(group * 32 + j * 8, 8), 8)
        f = [fsum[me.xl, i, rows, :] for i in range(8)] + [fother[i, rows, :] for i in range(8)]
        weighted = jnp.where(lane < VARS, small[2, point, :] / VARS, 0.0)
        goal = small[1, point, :]
        signs = [jnp.zeros((8, 128), F32) for _ in range(MEMBERS)]
        pairs = jnp.zeros((8, 128), F32)
        for a in range(MEMBERS):
            for b in range(a + 1, MEMBERS):
                d = f[a] - f[b]
                q = d * d + SMOOTH
                inv = lax.rsqrt(q)
                pairs = pairs + q * inv
                sl = d * inv
                signs[a] = signs[a] + sl
                signs[b] = signs[b] - sl
        misfits = jnp.zeros((8, 128), F32)
        for a in range(MEMBERS):
            d = f[a] - goal
            q = d * d + SMOOTH
            inv = lax.rsqrt(q)
            misfits = misfits + q * inv
            grad = (SCALE * weighted) * ((d * inv) * (1.0 / MEMBERS) - PAIR * signs[a])
            r["small_g"][a, rows, :] = grad
        term = misfits * (1.0 / MEMBERS) - PAIR * (pairs + MEMBERS * 0.5 * 0.2)
        r["loss_s"][0] += weighted * term

    for a in range(8):
        gf[a, group] = r["small_g"][a].astype(BF16)
        gfo[a] = r["small_g"][8 + a].astype(BF16)
    gs = [
        c.send(gfo, gf.at[:, group], r["g_ss"].at[0], r["g_rs"].at[0], me.pair_peer()),
        c.send(gfo, gf.at[:, group], r["g_ss"].at[1], r["g_rs"].at[1], me.cross_peer()),
        c.send(gf.at[:, group], gf.at[:, group], r["g_ss"].at[2], r["g_rs"].at[2], me.core_peer()),
    ]

    loss_s, loss_r = r["loss_s"], r["loss_r"]
    loss_pending = []

    def loss_send(level):
        if level == 0:
            loss_pending.append(
                [c.send(loss_s.at[0], loss_r.at[0], r["l_ss"].at[0], r["l_rs"].at[0], me.core_peer())]
            )
            return
        axis = "yzx"[level - 1]
        loss_pending.append(
            [
                c.send(
                    loss_s.at[level], loss_r.at[3 * level - 3 + i], r["l_ss"].at[3 * level - 3 + i],
                    r["l_rs"].at[3 * level - 3 + i], me.peer(axis, i),
                )
                for i in (1, 2, 3)
            ]
        )

    def loss_next(level):
        arrive(loss_pending[level])
        if level == 0:
            loss_s[1] = loss_s[0] + loss_r[0]
            return
        v = me.at("yzx"[level - 1])
        base = 3 * level - 3
        own, one, two, three = loss_s[level], loss_r[base + 1], loss_r[base + 2], loss_r[base + 3]
        total = (own + two) + (one + three)
        if level < 3:
            loss_s[level + 1] = total
        else:
            loss_o[...] = total

    loss_send(0)
    arrive(gs)
    gf_rows = gf[...].reshape(1024, 128)
    r["gf_t"][...] = gf_rows.T

    sb1, rb1, q1, sb2, rb2, q2, sb3, rb3, fin, obuf = (
        r[k] for k in ("sb1", "rb1", "q1", "sb2", "rb2", "q2", "sb3", "rb3", "fin", "obuf")
    )
    flight = {}

    def pick(axis, axes, value, cols):
        return tuple(value if a == axis else slice(None) for a in axes) + (slice(None), cols)

    def scatter_send(k, stage):
        c0, cw = ALL_PARTS[k]
        cols, order = pl.ds(c0, cw), ALL_ORDERS[k]
        axis = order[stage]
        axes = [a for a in "yzx" if a not in order[:stage]]
        src, dst = ((sb1, rb1), (sb2, rb2), (sb3, rb3))[stage]
        flight[k] = []
        for i in (2, 1, 3):
            there = (me.at(axis) + i) % 4
            flight[k].append(
                c.send(
                    src.at[pick(axis, axes, there, cols)],
                    dst.at[(i - 1,) + (slice(None),) * (3 - stage) + (cols,)],
                    r["rs_ss"].at[k, stage, i - 1], r["rs_rs"].at[k, stage, i - 1], me.peer(axis, i),
                )
            )

    def scatter_add(k, stage):
        c0, cw = ALL_PARTS[k]
        cols, order = slice(c0, c0 + cw), ALL_ORDERS[k]
        axis = order[stage]
        axes = [a for a in "yzx" if a not in order[:stage]]
        arrive(flight[k])
        own = (big, q1, q2)[stage]
        dst = (rb1, rb2, rb3)[stage]
        where = me.at(axis)
        if stage == 2:
            total = own[where, :, cols]
            for i in range(3):
                total = total + dst[i, :, cols].astype(F32)
            return total
        spot = axes.index(axis)
        keep, send = ((q1, sb2), (q2, sb3))[stage]
        for v in range(4):
            if stage == 0:
                index = [v, slice(None)]
                index.insert(spot, where)
                total = own[tuple(index) + (slice(None), cols)]
                for i in range(3):
                    total = total + dst[i, v, :, :, cols].astype(F32)
                keep[v, :, :, cols] = total
                send[v, :, :, cols] = total.astype(BF16)
            else:
                index = [v]
                index.insert(spot, where)
                total = own[tuple(index) + (slice(None), cols)]
                for i in range(3):
                    total = total + dst[i, v, :, cols].astype(F32)
                keep[v, :, cols] = total
                send[v, :, cols] = total.astype(BF16)

    def advance(k, stage):
        scatter_add(k, stage)
        scatter_send(k, stage + 1)

    finals = {}

    def finish(k):
        c0, cw = PARTS[k]
        total = scatter_add(k, 2) * (1.0 / SCALE)
        fin[me.xl, me.core, :, c0 : c0 + cw] = total
        here = fin.at[me.xl, me.core, :, pl.ds(c0, cw)]
        finals[k] = [
            c.send(here, here, r["fin_ss"].at[k, i], r["fin_rs"].at[k, i], d)
            for i, d in enumerate((me.pair_peer(), me.cross_peer(), me.core_peer()))
        ]

    out_flight = {}

    def out_stage(part, stage):
        order = ("yzx", "xyz")[part]
        c0 = 128 * part
        if stage == 0:
            total = scatter_add(6 + part, 2)
            obuf[me.core, me.y, me.z, me.x, :, c0 : c0 + 128] = total.astype(BF16)
        else:
            arrive(out_flight[part])
        if stage == 3:
            return
        index = (me.core,)
        index += tuple(pl.ds(0, 4) if a in order[:stage] else pl.ds(me.at(a), 1) for a in "yzx")
        index += (slice(None), pl.ds(c0, 128))
        out_flight[part] = [
            c.send(
                obuf.at[index], obuf.at[index], r["oa_ss"].at[part, stage, i - 1], r["oa_rs"].at[part, stage, i - 1],
                me.peer(order[stage], i),
            )
            for i in (2, 1, 3)
        ]

    for hg in range(8):
        part = dot(r["gf_t"][...], hid[:, 256 * hg : 256 * hg + 256])
        for vg in range(8):
            b = vg * 8 + hg
            block = part[16 * vg : 16 * vg + 16]
            big[b // 16, (b // 4) % 4, b % 4, :, HALF:WIDE] = block
            sb1[b // 16, (b // 4) % 4, b % 4, :, HALF:WIDE] = block.astype(BF16)
    scatter_send(6, 0)
    scatter_send(7, 0)

    def column_part(k):
        c0, cw = PARTS[k]
        cols = slice(c0, c0 + cw)
        for h in range(4):
            back = dot(gf[2 * h : 2 * h + 2].reshape(256, 128), wo[:, cols])
            slope = big[h, :, :, :, cols].reshape(256, cw)
            gpre[256 * h : 256 * h + 256, cols] = (back * slope).astype(BF16)
        for y in range(4):
            grad = dot(n_t[256 * y : 256 * y + 256, :], gpre[:, cols]).reshape(4, 4, 16, cw)
            big[y, :, :, :, cols] = grad
            sb1[y, :, :, :, cols] = grad.astype(BF16)
        scatter_send(k, 0)

    column_part(0)
    loss_next(0)
    loss_send(1)
    advance(6, 0)
    advance(7, 0)
    column_part(1)
    column_part(2)
    advance(0, 0)
    loss_next(1)
    loss_send(2)
    advance(6, 1)
    advance(7, 1)
    column_part(3)
    advance(1, 0)
    column_part(4)
    advance(2, 0)
    advance(0, 1)
    loss_next(2)
    loss_send(3)
    out_stage(0, 0)
    out_stage(1, 0)
    column_part(5)
    advance(3, 0)
    advance(1, 1)

    gno, gns, gnr = r["gno"], r["gns"], r["gnr"]
    theirs = pl.multiple_of((1 - me.core) * 512, 512)
    mine = pl.multiple_of(me.core * 512, 512)
    for n in range(4):
        part = dot(gpre[pl.ds(theirs, 512), :], wbuf[n].reshape(256, HALF), ((1,), (1,)))
        gns[:, :, 256 * n : 256 * n + 256] = part.reshape(4, 128, 256).astype(BF16)
    gn = [c.send(gns.at[i], gnr.at[i], r["gn_ss"].at[i], r["gn_rs"].at[i], me.core_peer()) for i in range(4)]
    advance(4, 0)
    advance(2, 1)
    out_stage(0, 1)
    out_stage(1, 1)
    finish(0)
    for n in range(4):
        part = dot(gpre[pl.ds(mine, 512), :], wbuf[n].reshape(256, HALF), ((1,), (1,)))
        gno[:, :, 256 * n : 256 * n + 256] = part.reshape(4, 128, 256)
    advance(5, 0)
    advance(3, 1)
    finish(1)
    out_stage(0, 2)
    out_stage(1, 2)

    for i in range(4):
        scale = 1.0 + ntab[pl.ds(seed[i], 1), :]
        gn[i].wait_recv()

        @pl.loop(0, 4)
        def _(j):
            rows = pl.ds(pl.multiple_of(j * 32, 32), 32)
            g = (gno[i, rows, :] + gnr[i, rows, :].astype(F32)) * scale
            unit = xhat[i, rows, :]
            m1 = jnp.mean(g, axis=-1, keepdims=True)
            m2 = jnp.mean(g * unit, axis=-1, keepdims=True)
            inv = jnp.mean(rstd[i, rows, :], axis=-1, keepdims=True)
            xhat[i, rows, :] = inv * (g - m1 - unit * m2)

        rows = dot(tab[0:32, :], xhat[i], precision=lax.Precision.HIGHEST)
        gl_o[i] = rows[0:16]
        r["rim_s"][0, 4 * i : 4 * i + 4, :] = rows[16:20]
        r["rim_s"][1, 4 * i : 4 * i + 4, :] = rows[20:24]
        if i == 1:
            advance(4, 1)
            finish(2)
    rims = [
        c.send(r["rim_s"].at[0], r["rim_r"].at[0], r["rim_ss"].at[0], r["rim_rs"].at[0], me.shard(-1)),
        c.send(r["rim_s"].at[1], r["rim_r"].at[1], r["rim_ss"].at[1], r["rim_rs"].at[1], me.shard(1)),
    ]
    advance(5, 1)
    finish(3)
    loss_next(3)
    out_stage(0, 3)
    out_stage(1, 3)
    own_out = obuf.at[me.core]
    oc = c.send(own_out, own_out, r["oc_ss"], r["oc_rs"], me.core_peer())
    finish(4)
    arrive(rims)
    for i in range(4):
        gl_o[i, 12:16, :] += r["rim_r"][0, 4 * i : 4 * i + 4, :] * has_next
        gl_o[i, 0:4, :] += r["rim_r"][1, 4 * i : 4 * i + 4, :] * has_prev
    oc.wait_recv()
    for core in range(2):
        for b in range(56):
            vg, hg = b // 8, b % 8
            rows = min(16, VARS - 16 * vg)
            block = obuf[core, b // 16, (b // 4) % 4, b % 4].astype(F32) * (1.0 / SCALE)
            at = core * HALF + 256 * hg
            gwo_o[16 * vg : 16 * vg + rows, at : at + 256] = block[0:rows]
    finish(5)
    for k in range(6):
        arrive(finals[k])
    for xl in range(2):
        for core in range(2):
            gwi_o[16 * xl : 16 * xl + 16, HALF * core : HALF * core + HALF] = fin[xl, core]
    c.drain()


SCRATCH["small_g"] = pltpu.VMEM((16, 32, 128), F32)


def local(latent, edge_index, edge_weight, noise_seed, noise_table, w_in, w_out, target, area_weight):
    vmem = pl.BlockSpec(memory_space=pltpu.VMEM)
    smem = pl.BlockSpec(memory_space=pltpu.SMEM)
    loss, grad_latent, grad_in, grad_out = pl.pallas_call(
        kernel,
        out_shape=(
            jax.ShapeDtypeStruct((8, 128), F32),
            jax.ShapeDtypeStruct((4, 16, LAT), F32),
            jax.ShapeDtypeStruct((32, 2 * HALF), F32),
            jax.ShapeDtypeStruct((VARS, 2 * HALF), F32),
        ),
        in_specs=[vmem, vmem, vmem, smem] + [vmem] * 5,
        out_specs=(vmem,) * 4,
        scratch_shapes=list(SCRATCH.values()),
        compiler_params=pltpu.CompilerParams(
            collective_id=0, has_side_effects=True, vmem_limit_bytes=63 * 2**20
        ),
    )(latent, edge_index, edge_weight, noise_seed, noise_table, w_in, w_out, target, area_weight.reshape(1, -1))
    return (jnp.sum(loss) / POINTS, grad_latent, grad_in, grad_out)


def solution(mesh):
    return jax.shard_map(
        local,
        mesh=mesh,
        in_specs=(
            P("member", "space", None),
            P(None, "space"),
            P(None, "space"),
            P("member"),
            P(),
            P("space", None),
            P(),
            P(None, "space"),
            P("space"),
        ),
        out_specs=(P(), P("member", "space", None), P("space", None), P()),
        check_vma=False,
    )
```

```python
import jax
import jax.numpy as jnp
from jax import lax
from jax.experimental import pallas as pl
from jax.experimental.pallas import tpu as pltpu
from jax.sharding import PartitionSpec as P

VARS = 100
HALO = 4
MEMBERS = 16
POINTS = 4096
F32 = jnp.float32
BF16 = jnp.bfloat16
EPS = 1e-05
SMOOTH = 0.04
SCALE = 1024.0
PAIR = 1.0 / (MEMBERS * (MEMBERS - 1))
GELU_C = 0.7978845608028654
MESH = pl.DeviceIdType.MESH

LAT = 1024
HALF = 2048
WIDE = HALF + 256
GROUPS = [
    ("yzx", 0, 384),
    ("zyx", 384, 384),
    ("xzy", 768, 384),
    ("zxy", 1152, 384),
    ("xyz", 1536, 256),
    ("yxz", 1792, 256),
]
SEND_ORDER = (0, 2, 4, 1, 3, 5)
CHUNKS = [(0, (0,)), (768, (2,)), (1536, (4,)), (256, (0, 1)), (512, (1,)), (1024, (2, 3)), (1280, (3,)), (1792, (5,))]
PARTS = [(0, 256), (256, 256), (1536, 512), (512, 512), (1024, 512), (2048, 256)]
ORDERS = ["xyz", "yzx", "zyx", "xzy", "yxz", "zxy"]
X1, Y1, Z2, X2, Y2, OUT = range(6)

DMA = pltpu.SemaphoreType.DMA
SCRATCH = dict(
    wbuf=pltpu.VMEM((4, 4, 4, 16, HALF), BF16),
    wo=pltpu.VMEM((128, HALF), BF16),
    wo_t=pltpu.VMEM((HALF, 128), BF16),
    nbuf=pltpu.VMEM((4, 8, 32, LAT), BF16),
    n_t=pltpu.VMEM((LAT, 1024), BF16),
    xhat=pltpu.VMEM((4, 128, LAT), F32),
    rstd=pltpu.VMEM((4, 128, 128), F32),
    tab=pltpu.VMEM((128, 128), F32),
    small=pltpu.VMEM((3, 128, 128), F32),
    hid=pltpu.VMEM((4, 256, HALF), BF16),
    big=pltpu.VMEM((4, 4, 4, 16, WIDE), F32),
    gpre=pltpu.VMEM((4, 256, HALF), BF16),
    halo_s=pltpu.VMEM((2, 16, LAT), BF16),
    halo_r=pltpu.VMEM((4, 16, LAT), BF16),
    fpart=pltpu.VMEM((4, 8, 32, 128), F32),
    fcore=pltpu.VMEM((2, 8, 32, 128), F32),
    fsum=pltpu.VMEM((2, 8, 32, 128), F32),
    fother=pltpu.VMEM((8, 32, 128), F32),
    gf=pltpu.VMEM((4, 8, 32, 128), BF16),
    gfo=pltpu.VMEM((8, 32, 128), BF16),
    gf_t=pltpu.VMEM((128, 1024), BF16),
    sb1=pltpu.VMEM((4, 4, 4, 16, WIDE), BF16),
    rb1=pltpu.VMEM((3, 4, 4, 16, WIDE), BF16),
    q1=pltpu.VMEM((4, 4, 16, WIDE), F32),
    sb2=pltpu.VMEM((4, 4, 16, WIDE), BF16),
    rb2=pltpu.VMEM((3, 4, 16, WIDE), BF16),
    q2=pltpu.VMEM((4, 16, WIDE), F32),
    sb3=pltpu.VMEM((4, 16, WIDE), BF16),
    rb3=pltpu.VMEM((3, 16, WIDE), BF16),
    fin=pltpu.VMEM((2, 2, 16, HALF), F32),
    obuf=pltpu.VMEM((2, 4, 4, 4, 16, 256), BF16),
    gno=pltpu.VMEM((4, 4, 32, LAT), F32),
    gns=pltpu.VMEM((4, 4, 32, LAT), BF16),
    gnr=pltpu.VMEM((4, 4, 32, LAT), BF16),
    rim_s=pltpu.VMEM((2, 16, LAT), F32),
    rim_r=pltpu.VMEM((4, 16, LAT), F32),
    gwo=pltpu.VMEM((VARS, 2 * HALF), F32),
    glat=pltpu.VMEM((4, 16, LAT), F32),
    out_sem=DMA((6,)),
    loss_s=pltpu.VMEM((4, 8, 128), F32),
    loss_r=pltpu.VMEM((10, 8, 128), F32),
    ag_ss=DMA((18, 3)),
    ag_rs=DMA((18, 3)),
    rs_ss=DMA((6, 3, 3)),
    rs_rs=DMA((6, 3, 3)),
    oa_ss=DMA((2, 3, 3)),
    oa_rs=DMA((2, 3, 3)),
    fin_ss=DMA((5, 3)),
    fin_rs=DMA((5, 3)),
    n_ss=DMA((4,)),
    n_rs=DMA((4,)),
    gn_ss=DMA((4,)),
    gn_rs=DMA((4,)),
    halo_ss=DMA((3,)),
    halo_rs=DMA((3,)),
    rim_ss=DMA((4,)),
    rim_rs=DMA((4,)),
    f_ss=DMA((2,)),
    f_rs=DMA((2,)),
    g_ss=DMA((3,)),
    g_rs=DMA((3,)),
    oc_ss=DMA,
    oc_rs=DMA,
    l_ss=DMA((10,)),
    l_rs=DMA((10,)),
)


def dot(a, b, dims=((1,), (0,)), precision=None):
    return lax.dot_general(a, b, (dims, ((), ())), precision=precision, preferred_element_type=F32)


class Place:
    def __init__(self):
        m, s = lax.axis_index("member"), lax.axis_index("space")
        self.m, self.s = m, s
        self.xl, self.core = m // 2, m % 2
        self.y, self.z, self.xh = s // 8, (s // 2) % 4, s % 2
        self.x = self.xh * 2 + self.xl
        self.turn = 1 - 2 * self.xh

    def device(self, y, z, x):
        return ((x % 2) * 2 + self.core, (y * 4 + z) * 2 + x // 2)

    def at(self, axis):
        return getattr(self, axis)

    def peer(self, axis, step):
        q = dict(y=self.y, z=self.z, x=self.x)
        q[axis] = (q[axis] + step) % 4
        return self.device(**q)

    def core_peer(self):
        return (self.xl * 2 + 1 - self.core, self.s)

    def pair_peer(self):
        return ((1 - self.xl) * 2 + self.core, self.s)

    def cross_peer(self):
        return ((1 - self.xl) * 2 + 1 - self.core, self.s)


class Copies:
    def __init__(self):
        self.sent = []

    def send(self, src, dst, ss, rs, device):
        copy = pltpu.make_async_remote_copy(
            src_ref=src, dst_ref=dst, send_sem=ss, recv_sem=rs, device_id=device, device_id_type=MESH
        )
        copy.start()
        self.sent.append(copy)
        return copy

    def drain(self):
        for copy in self.sent:
            copy.wait_send()


def arrive(copies):
    for copy in copies:
        copy.wait_recv()


def kernel(lat, eidx, ewt, seed, ntab, w_in, w_out, target, area, loss_o, gl_o, gwi_o, gwo_o, *refs):
    r = dict(zip(SCRATCH, refs))
    wbuf, big, nbuf, n_t, hid, gpre, wo = (r[k] for k in ("wbuf", "big", "nbuf", "n_t", "hid", "gpre", "wo"))
    xhat, rstd, tab, small = r["xhat"], r["rstd"], r["tab"], r["small"]
    me = Place()
    c = Copies()
    col0 = pl.multiple_of(me.core * HALF, 128)

    friends = [me.peer(a, k) for a in "yzx" for k in (1, 2, 3)]
    friends += [me.core_peer(), me.cross_peer()]
    barrier = pltpu.get_barrier_semaphore()
    for d in friends:
        pl.semaphore_signal(barrier, inc=1, device_id=d, device_id_type=MESH)

    wbuf[me.y, me.z, me.x] = w_in[pl.ds(pl.multiple_of(me.xl * 16, 16), 16), pl.ds(col0, HALF)]
    lat32 = [lat[i].astype(F32) for i in range(4)]
    r["halo_s"][0] = jnp.concatenate([v[12:16] for v in lat32], axis=0).astype(BF16)
    r["halo_s"][1] = jnp.concatenate([v[0:4] for v in lat32], axis=0).astype(BF16)
    pl.semaphore_wait(barrier, len(friends))

    halo_s, halo_r = r["halo_s"], r["halo_r"]

    def halo_send(src, dst, k, device):
        return c.send(src, dst, r["halo_ss"].at[k], r["halo_rs"].at[k], device)

    halo = [halo_send(halo_s, halo_r.at[pl.ds(0, 2)], 0, me.peer("x", 2))]

    def gather_send(slot, group, stage, c0, cw):
        order = GROUPS[group][0]
        index = tuple(pl.ds(0, 4) if a in order[:stage] else pl.ds(me.at(a), 1) for a in "yzx")
        index += (slice(None), pl.ds(c0, cw))
        here = wbuf.at[index]
        return [
            c.send(here, here, r["ag_ss"].at[slot, i - 1], r["ag_rs"].at[slot, i - 1], me.peer(order[stage], i))
            for i in (2, 1, 3)
        ]

    gathered = {}

    def gather_stage(stage):
        for g in SEND_ORDER:
            _, c0, cw = GROUPS[g]
            arrive(gathered.pop(g, []))
            gathered[g] = gather_send(6 * stage + g, g, stage, c0, cw)

    gather_stage(0)

    node = lax.broadcasted_iota(jnp.int32, (128, 128), 0)
    row_of = jnp.where(node < 16, node + HALO, jnp.where(node < 20, node - 16, jnp.where(node < 24, node, -1)))
    table_t = jnp.zeros((128, 128), F32)
    for k in range(3):
        table_t = table_t + jnp.where(row_of == eidx[k : k + 1, :], ewt[k : k + 1, :], 0.0)
    tab[...] = table_t
    table = table_t.T[:, :32]
    t_hi = table.astype(BF16)
    t_rest = table - t_hi.astype(F32)
    t_mid = t_rest.astype(BF16)
    t_low = (t_rest - t_mid.astype(F32)).astype(BF16)
    small[0] = jnp.zeros((128, 128), F32)
    small[0, 0:VARS] = target[...]
    small[1] = small[0].T
    small[2] = jnp.broadcast_to(area[...], (128, 128)).T

    arrive(halo)
    halo = [halo_send(halo_r.at[me.xh], halo_r.at[2], 1, me.peer("z", me.turn))]
    gather_stage(1)
    arrive(halo)
    halo = [halo_send(halo_r.at[2], halo_r.at[3], 2, me.peer("y", me.turn))]
    big[0, 0:2, :, :, 0:HALF] = jnp.zeros((2, 4, 16, HALF), F32)
    head = w_out[:, pl.ds(col0, HALF)].astype(F32)
    for v in range(6):
        big[0, v // 4, v % 4, :, 0:HALF] = head[16 * v : 16 * v + 16]
    big[0, 1, 2, 0:4, 0:HALF] = head[96:100]
    wo[...] = big[0, 0:2, :, :, 0:HALF].reshape(128, HALF).astype(BF16)
    r["wo_t"][...] = wo[...].T

    gather_stage(2)

    arrive(halo)
    has_prev = (me.s > 0).astype(F32)
    has_next = (me.s < 31).astype(F32)
    prev_at = jnp.where(me.xh == 0, jnp.where(me.z == 0, 3, 2), 0)
    next_at = jnp.where(me.xh == 1, jnp.where(me.z == 3, 3, 2), 1)
    prev_rows = halo_r[prev_at].astype(F32) * has_prev
    next_rows = halo_r[next_at].astype(F32) * has_next
    normed = []
    for i in range(4):
        edges = [lat[i].astype(F32), prev_rows[4 * i : 4 * i + 4], next_rows[4 * i : 4 * i + 4]]
        window = jnp.concatenate(edges + [jnp.zeros((8, LAT), F32)], axis=0).astype(BF16)
        xhat[i] = dot(t_hi, window) + dot(t_mid, window) + dot(t_low, window)
        scale = 1.0 + ntab[pl.ds(seed[i], 1), :]
        row = me.core * 4 + i

        @pl.loop(0, 4)
        def _(j):
            rows = pl.ds(pl.multiple_of(j * 32, 32), 32)
            a = xhat[i, rows, :]
            centred = a - jnp.mean(a, axis=-1, keepdims=True)
            inv = lax.rsqrt(jnp.mean(centred * centred, axis=-1, keepdims=True) + EPS)
            unit = centred * inv
            xhat[i, rows, :] = unit
            rstd[i, rows, :] = jnp.broadcast_to(inv, (32, 128))
            nbuf[j, row] = (unit * scale).astype(BF16)

        normed.append(c.send(nbuf.at[:, row], nbuf.at[:, row], r["n_ss"].at[i], r["n_rs"].at[i], me.core_peer()))
    arrive(normed)
    for g in range(4):
        n_t[:, 256 * g : 256 * g + 256] = nbuf[g].reshape(256, LAT).T

    fpart, fcore, fsum, fother, gf, gfo = (r[k] for k in ("fpart", "fcore", "fsum", "fother", "gf", "gfo"))
    fpart[...] = jnp.zeros_like(fpart)
    for c0, sources in CHUNKS:
        for g in sources:
            arrive(gathered.pop(g, []))
        cols = slice(c0, c0 + 256)

        w = wbuf[:, :, :, :, cols].reshape(LAT, 256)
        for h in range(4):
            pre = dot(nbuf[h].reshape(256, LAT), w)
            sq = pre * pre
            t = jnp.tanh(pre * (GELU_C + (GELU_C * 0.044715) * sq))
            cdf = 0.5 + 0.5 * t
            act = (pre * cdf).astype(BF16)
            hid[h, :, cols] = act
            slope = cdf + (0.5 * pre) * (1.0 - t * t) * (GELU_C + (3.0 * GELU_C * 0.044715) * sq)
            big[h, :, :, :, cols] = slope.reshape(4, 4, 16, 256)
        for h in range(4):
            fpart[h] += dot(hid[h, :, cols], r["wo_t"][cols, :]).reshape(8, 32, 128)

    f1 = c.send(
        fpart.at[pl.ds(2 * (1 - me.core), 2)], fcore, r["f_ss"].at[0], r["f_rs"].at[0], me.core_peer()
    )
    f1.wait_recv()
    for g in range(2):
        fsum[g] = fpart[2 * me.core + g] + fcore[g]
    f2 = c.send(fsum.at[1 - me.xl], fother, r["f_ss"].at[1], r["f_rs"].at[1], me.pair_peer())
    group = me.core * 2 + me.xl
    f2.wait_recv()

    r["loss_s"][0] = jnp.zeros((8, 128), F32)
    lane = lax.broadcasted_iota(jnp.int32, (8, 128), 1)

    @pl.loop(0, 4)
    def _(j):
        rows = pl.ds(pl.multiple_of(j * 8, 8), 8)
        point = pl.ds(pl.multiple_of(group * 32 + j * 8, 8), 8)
        f = [fsum[me.xl, i, rows, :] for i in range(8)] + [fother[i, rows, :] for i in range(8)]
        weighted = jnp.where(lane < VARS, small[2, point, :] / VARS, 0.0)
        goal = small[1, point, :]
        signs = [jnp.zeros((8, 128), F32) for _ in range(MEMBERS)]
        pairs = jnp.zeros((8, 128), F32)
        for a in range(MEMBERS):
            for b in range(a + 1, MEMBERS):
                d = f[a] - f[b]
                q = d * d + SMOOTH
                inv = lax.rsqrt(q)
                pairs = pairs + q * inv
                sl = d * inv
                signs[a] = signs[a] + sl
                signs[b] = signs[b] - sl
        misfits = jnp.zeros((8, 128), F32)
        for a in range(MEMBERS):
            d = f[a] - goal
            q = d * d + SMOOTH
            inv = lax.rsqrt(q)
            misfits = misfits + q * inv
            grad = (SCALE * weighted) * ((d * inv) * (1.0 / MEMBERS) - PAIR * signs[a])
            r["small_g"][a, rows, :] = grad
        term = misfits * (1.0 / MEMBERS) - PAIR * (pairs + MEMBERS * 0.5 * 0.2)
        r["loss_s"][0] += weighted * term

    for a in range(8):
        gf[group, a] = r["small_g"][a].astype(BF16)
        gfo[a] = r["small_g"][8 + a].astype(BF16)
    gs = [
        c.send(gfo, gf.at[group], r["g_ss"].at[0], r["g_rs"].at[0], me.pair_peer()),
        c.send(gf.at[group], gf.at[group], r["g_ss"].at[1], r["g_rs"].at[1], me.core_peer()),
    ]

    loss_s, loss_r = r["loss_s"], r["loss_r"]
    loss_pending = []

    def loss_send(level):
        if level == 0:
            loss_pending.append(
                [c.send(loss_s.at[0], loss_r.at[0], r["l_ss"].at[0], r["l_rs"].at[0], me.core_peer())]
            )
            return
        axis = "yzx"[level - 1]
        loss_pending.append(
            [
                c.send(
                    loss_s.at[level], loss_r.at[3 * level - 3 + i], r["l_ss"].at[3 * level - 3 + i],
                    r["l_rs"].at[3 * level - 3 + i], me.peer(axis, i),
                )
                for i in (1, 2, 3)
            ]
        )

    def loss_next(level):
        arrive(loss_pending[level])
        if level == 0:
            loss_s[1] = loss_s[0] + loss_r[0]
            return
        v = me.at("yzx"[level - 1])
        base = 3 * level - 3
        own, one, two, three = loss_s[level], loss_r[base + 1], loss_r[base + 2], loss_r[base + 3]
        total = (own + two) + (one + three)
        if level < 3:
            loss_s[level + 1] = total
        else:
            loss_o[...] = total

    loss_send(0)

    def back(h):
        @pl.loop(0, 2)
        def _(j):
            for k in range(4):
                cols = pl.ds(pl.multiple_of(j * 1024 + k * 256, 256), 256)
                slope = big[h, :, :, :, cols].reshape(256, 256)
                gpre[h, :, cols] = (dot(gf[h].reshape(256, 128), wo[:, cols]) * slope).astype(BF16)

    back(group)
    gs[1].wait_recv()
    back((1 - me.core) * 2 + me.xl)
    pair = me.core * 2 + 1 - me.xl
    gs[0].wait_recv()
    gs.append(c.send(gf.at[pair], gf.at[pair], r["g_ss"].at[2], r["g_rs"].at[2], me.core_peer()))
    back(pair)
    gs[2].wait_recv()
    back((1 - me.core) * 2 + 1 - me.xl)
    r["gf_t"][...] = gf[...].reshape(1024, 128).T

    sb1, rb1, q1, sb2, rb2, q2, sb3, rb3, fin, obuf = (
        r[k] for k in ("sb1", "rb1", "q1", "sb2", "rb2", "q2", "sb3", "rb3", "fin", "obuf")
    )
    flight = {}

    def pick(axis, axes, value, cols):
        return tuple(value if a == axis else slice(None) for a in axes) + (slice(None), cols)

    def scatter_send(k, stage):
        c0, cw = PARTS[k]
        cols, order = pl.ds(c0, cw), ORDERS[k]
        axis = order[stage]
        axes = [a for a in "yzx" if a not in order[:stage]]
        src, dst = ((sb1, rb1), (sb2, rb2), (sb3, rb3))[stage]
        flight[k] = []
        for i in (2, 1, 3):
            there = (me.at(axis) + i) % 4
            flight[k].append(
                c.send(
                    src.at[pick(axis, axes, there, cols)],
                    dst.at[(i - 1,) + (slice(None),) * (3 - stage) + (cols,)],
                    r["rs_ss"].at[k, stage, i - 1], r["rs_rs"].at[k, stage, i - 1], me.peer(axis, i),
                )
            )

    def scatter_add(k, stage):
        c0, cw = PARTS[k]
        cols, order = slice(c0, c0 + cw), ORDERS[k]
        axis = order[stage]
        axes = [a for a in "yzx" if a not in order[:stage]]
        arrive(flight[k])
        own = (big, q1, q2)[stage]
        dst = (rb1, rb2, rb3)[stage]
        where = me.at(axis)
        if stage == 2:
            total = own[where, :, cols]
            for i in range(3):
                total = total + dst[i, :, cols].astype(F32)
            return total
        spot = axes.index(axis)
        keep, send = ((q1, sb2), (q2, sb3))[stage]
        for v in range(4):
            if stage == 0:
                index = [v, slice(None)]
                index.insert(spot, where)
                total = own[tuple(index) + (slice(None), cols)]
                for i in range(3):
                    total = total + dst[i, v, :, :, cols].astype(F32)
                keep[v, :, :, cols] = total
                send[v, :, :, cols] = total.astype(BF16)
            else:
                index = [v]
                index.insert(spot, where)
                total = own[tuple(index) + (slice(None), cols)]
                for i in range(3):
                    total = total + dst[i, v, :, cols].astype(F32)
                keep[v, :, cols] = total
                send[v, :, cols] = total.astype(BF16)

    def advance(k, stage):
        scatter_add(k, stage)
        scatter_send(k, stage + 1)

    finals = {}

    def final_send(k, i, xl, device):
        c0, cw = PARTS[k]
        here = fin.at[xl, me.core, :, pl.ds(c0, cw)]
        return c.send(here, here, r["fin_ss"].at[k, i], r["fin_rs"].at[k, i], device)

    def finish(k):
        c0, cw = PARTS[k]
        fin[me.xl, me.core, :, c0 : c0 + cw] = scatter_add(k, 2) * (1.0 / SCALE)
        finals[k] = [
            final_send(k, 0, me.xl, me.pair_peer()),
            final_send(k, 1, me.xl, me.core_peer()),
        ]

    def finish_pass(k):
        finals[k][0].wait_recv()
        finals[k][0] = final_send(k, 2, 1 - me.xl, me.core_peer())

    out_flight = {}

    def out_stage(part, stage):
        order = ("yzx", "xyz")[part]
        c0 = 128 * part
        if stage == 0:
            if part == 0:
                obuf[me.core, me.y, me.z, me.x] = scatter_add(OUT, 2).astype(BF16)
        else:
            arrive(out_flight[part])
        if stage == 3:
            return
        index = (me.core,)
        index += tuple(pl.ds(0, 4) if a in order[:stage] else pl.ds(me.at(a), 1) for a in "yzx")
        index += (slice(None), pl.ds(c0, 128))
        out_flight[part] = [
            c.send(
                obuf.at[index], obuf.at[index], r["oa_ss"].at[part, stage, i - 1], r["oa_rs"].at[part, stage, i - 1],
                me.peer(order[stage], i),
            )
            for i in (2, 1, 3)
        ]

    @pl.loop(0, 8)
    def _(hg):
        cols = pl.ds(pl.multiple_of(hg * 256, 256), 256)
        part = dot(r["gf_t"][...], hid[:, :, cols].reshape(1024, 256))
        for vg in range(8):
            block = part[16 * vg : 16 * vg + 16]
            y, z, x = vg // 2, (vg % 2) * 2 + hg // 4, hg % 4
            big[y, z, x, :, HALF:WIDE] = block
            sb1[y, z, x, :, HALF:WIDE] = block.astype(BF16)

    scatter_send(OUT, 0)

    def column_part(k):
        c0, cw = PARTS[k]
        for c1 in range(c0, c0 + cw, 256):
            cols = slice(c1, c1 + 256)
            for y in range(4):
                rows = slice(256 * y, 256 * y + 256)
                grad = dot(n_t[rows, :], gpre[:, :, cols].reshape(1024, 256)).reshape(4, 4, 16, 256)
                big[y, :, :, :, cols] = grad
                sb1[y, :, :, :, cols] = grad.astype(BF16)
        scatter_send(k, 0)

    gno, gns, gnr = r["gno"], r["gns"], r["gnr"]

    def grad_normed(core, dst):
        members = pl.ds(pl.multiple_of(core * 128, 128), 128)

        @pl.loop(0, 4)
        def _(n):
            lanes = pl.ds(pl.multiple_of(n * 256, 256), 256)
            part = dot(gpre[:, members, :].reshape(512, HALF), wbuf[n].reshape(256, HALF), ((1,), (1,)))
            dst[:, :, :, lanes] = part.reshape(4, 4, 32, 256).astype(dst.dtype)

    glat, rim_s, rim_r = r["glat"], r["rim_s"], r["rim_r"]

    def norm_back(i):
        scale = 1.0 + ntab[pl.ds(seed[i], 1), :]
        gn[i].wait_recv()
        for j in range(4):
            rows = slice(32 * j, 32 * j + 32)
            g = (gno[j, i] + gnr[j, i].astype(F32)) * scale
            unit = xhat[i, rows, :]
            m1 = jnp.mean(g, axis=-1, keepdims=True)
            m2 = jnp.mean(g * unit, axis=-1, keepdims=True)
            inv = rstd[i, rows, :][:, 0:1]
            xhat[i, rows, :] = inv * (g - m1 - unit * m2)
        rows = dot(tab[0:32, :], xhat[i], precision=lax.Precision.HIGHEST)
        glat[i] = rows[0:16]
        rim_s[0, 4 * i : 4 * i + 4, :] = rows[16:20]
        rim_s[1, 4 * i : 4 * i + 4, :] = rows[20:24]

    def rim_send(src, dst, k, device):
        return c.send(src, dst, r["rim_ss"].at[k], r["rim_rs"].at[k], device)

    for k in (X1, Y1, Z2, X2, Y2):
        column_part(k)
        if k == Y1:
            loss_next(0)
            loss_send(1)
    grad_normed(1 - me.core, gns)
    gn = [c.send(gns.at[:, i], gnr.at[:, i], r["gn_ss"].at[i], r["gn_rs"].at[i], me.core_peer()) for i in range(4)]
    for k in (OUT, X1, Y1):
        advance(k, 0)
    loss_next(1)
    loss_send(2)
    grad_normed(me.core, gno)
    norm_back(0)
    norm_back(1)
    for k in (OUT, X1, Y1):
        advance(k, 1)
    loss_next(2)
    loss_send(3)
    norm_back(2)
    norm_back(3)
    near = rim_send(rim_s.at[1 - me.xh], rim_r.at[0], 0, me.peer("x", 2))
    far = rim_send(rim_s.at[me.xh], rim_r.at[1], 1, me.peer("z", -me.turn))
    out_stage(0, 0)
    out_stage(1, 0)
    finish(X1)
    finish(Y1)
    for k in (Z2, X2, Y2):
        advance(k, 0)
    far.wait_recv()
    far = rim_send(rim_r.at[1], rim_r.at[2], 2, me.peer("y", -me.turn))
    out_stage(0, 1)
    out_stage(1, 1)
    for k in (Z2, X2, Y2):
        advance(k, 1)
    far.wait_recv()
    carried = jnp.where(me.xh == 0, me.z == 3, me.z == 0)
    last = rim_send(rim_r.at[jnp.where(carried, 2, 1)], rim_r.at[3], 3, me.peer("x", 2))
    out_stage(0, 2)
    out_stage(1, 2)
    for k in (Z2, X2, Y2):
        finish(k)
    for k in (X1, Y1):
        finish_pass(k)
    loss_next(3)
    out_stage(0, 3)
    out_stage(1, 3)
    own_out = obuf.at[me.core]
    oc = c.send(own_out, own_out, r["oc_ss"], r["oc_rs"], me.core_peer())
    near.wait_recv()
    last.wait_recv()
    from_next = rim_r[jnp.where(me.xh == 0, 0, 3)] * has_next
    from_prev = rim_r[jnp.where(me.xh == 0, 3, 0)] * has_prev
    for i in range(4):
        glat[i, 12:16, :] += from_next[4 * i : 4 * i + 4]
        glat[i, 0:4, :] += from_prev[4 * i : 4 * i + 4]
    leave = [pltpu.make_async_copy(glat, gl_o, r["out_sem"].at[0])]
    leave[0].start()
    for k in (Z2, X2, Y2):
        finish_pass(k)
    oc.wait_recv()
    gwo = r["gwo"]
    for core in range(2):
        for b in range(56):
            vg, hg = b // 8, b % 8
            rows = min(16, VARS - 16 * vg)
            block = obuf[core, b // 16, (b // 4) % 4, b % 4].astype(F32) * (1.0 / SCALE)
            at = core * HALF + 256 * hg
            gwo[16 * vg : 16 * vg + rows, at : at + 256] = block[0:rows]
    leave.append(pltpu.make_async_copy(gwo, gwo_o, r["out_sem"].at[1]))
    leave[1].start()
    for k in finals:
        arrive(finals[k])
    for xl in range(2):
        for core in range(2):
            dst = gwi_o.at[pl.ds(16 * xl, 16), pl.ds(HALF * core, HALF)]
            leave.append(pltpu.make_async_copy(fin.at[xl, core], dst, r["out_sem"].at[2 + 2 * xl + core]))
            leave[-1].start()
    for copy in leave:
        copy.wait()
    c.drain()


SCRATCH["small_g"] = pltpu.VMEM((16, 32, 128), F32)


def hand_on(loss, gl, gwi, gwo, loss_o, gl_o, gwi_o, gwo_o):
    loss_o[0, 0] = jnp.sum(loss[...]) * (1.0 / POINTS)
    gl_o[...] = gl[...]
    gwi_o[...] = gwi[...]
    gwo_o[...] = gwo[...]


def local(latent, edge_index, edge_weight, noise_seed, noise_table, w_in, w_out, target, area_weight):
    vmem = pl.BlockSpec(memory_space=pltpu.VMEM)
    smem = pl.BlockSpec(memory_space=pltpu.SMEM)
    anywhere = pl.BlockSpec(memory_space=pl.ANY)
    grads = (
        jax.ShapeDtypeStruct((4, 16, LAT), F32),
        jax.ShapeDtypeStruct((32, 2 * HALF), F32),
        jax.ShapeDtypeStruct((VARS, 2 * HALF), F32),
    )
    made = pl.pallas_call(
        kernel,
        out_shape=(jax.ShapeDtypeStruct((8, 128), F32),) + grads,
        in_specs=[vmem, vmem, vmem, smem] + [vmem] * 5,
        out_specs=(vmem,) + (anywhere,) * 3,
        scratch_shapes=list(SCRATCH.values()),
        compiler_params=pltpu.CompilerParams(
            collective_id=0, has_side_effects=True, vmem_limit_bytes=63 * 2**20
        ),
    )(latent, edge_index, edge_weight, noise_seed, noise_table, w_in, w_out, target, area_weight.reshape(1, -1))
    loss, grad_latent, grad_in, grad_out = pl.pallas_call(
        hand_on,
        out_shape=(jax.ShapeDtypeStruct((1, 1), F32),) + grads,
        in_specs=[vmem] * 4,
        out_specs=(smem,) + (vmem,) * 3,
    )(*made)
    return (loss[0, 0], grad_latent, grad_in, grad_out)


def solution(mesh):
    return jax.shard_map(
        local,
        mesh=mesh,
        in_specs=(
            P("member", "space", None),
            P(None, "space"),
            P(None, "space"),
            P("member"),
            P(),
            P("space", None),
            P(),
            P(None, "space"),
            P("space"),
        ),
        out_specs=(P(), P("member", "space", None), P("space", None), P()),
        check_vma=False,
    )
```

```python
import jax
import jax.numpy as jnp
from jax import lax
from jax.experimental import pallas as pl
from jax.experimental.pallas import tpu as pltpu
from jax.sharding import PartitionSpec as P

VARS = 100
HALO = 4
MEMBERS = 16
POINTS = 4096
F32 = jnp.float32
BF16 = jnp.bfloat16
EPS = 1e-05
SMOOTH = 0.04
SCALE = 1024.0
PAIR = 1.0 / (MEMBERS * (MEMBERS - 1))
GELU_C = 0.7978845608028654
MESH = pl.DeviceIdType.MESH

LAT = 1024
HALF = 2048
WIDE = HALF + 256
GROUPS = [
    ("yzx", 0, 384),
    ("zyx", 384, 384),
    ("xzy", 768, 384),
    ("zxy", 1152, 384),
    ("xyz", 1536, 256),
    ("yxz", 1792, 256),
]
SEND_ORDER = (0, 2, 4, 1, 3, 5)
CHUNKS = [(0, (0,)), (768, (2,)), (1536, (4,)), (256, (0, 1)), (512, (1,)), (1024, (2, 3)), (1280, (3,)), (1792, (5,))]
PARTS = [(0, 256), (256, 256), (1536, 512), (512, 512), (1024, 512), (2048, 256)]
ORDERS = ["xyz", "yzx", "zyx", "xzy", "yxz", "zxy"]
X1, Y1, Z2, X2, Y2, OUT = range(6)

DMA = pltpu.SemaphoreType.DMA
SCRATCH = dict(
    wbuf=pltpu.VMEM((4, 4, 4, 16, HALF), BF16),
    wo=pltpu.VMEM((128, HALF), BF16),
    wo_t=pltpu.VMEM((HALF, 128), BF16),
    nbuf=pltpu.VMEM((4, 8, 32, LAT), BF16),
    n_t=pltpu.VMEM((LAT, 1024), BF16),
    xhat=pltpu.VMEM((4, 128, LAT), F32),
    rstd=pltpu.VMEM((4, 128, 128), F32),
    tab=pltpu.VMEM((128, 128), F32),
    small=pltpu.VMEM((3, 128, 128), F32),
    hid=pltpu.VMEM((4, 256, HALF), BF16),
    big=pltpu.VMEM((4, 4, 4, 16, WIDE), F32),
    gpre=pltpu.VMEM((4, 256, HALF), BF16),
    halo_s=pltpu.VMEM((2, 16, LAT), BF16),
    halo_r=pltpu.VMEM((4, 16, LAT), BF16),
    fpart=pltpu.VMEM((4, 8, 32, 128), F32),
    fcore=pltpu.VMEM((2, 8, 32, 128), F32),
    fsum=pltpu.VMEM((2, 8, 32, 128), F32),
    fother=pltpu.VMEM((8, 32, 128), F32),
    gf=pltpu.VMEM((4, 8, 32, 128), BF16),
    gfo=pltpu.VMEM((8, 32, 128), BF16),
    gf_t=pltpu.VMEM((128, 1024), BF16),
    sb1=pltpu.VMEM((4, 4, 4, 16, WIDE), BF16),
    rb1=pltpu.VMEM((2, 4, 4, 16, WIDE), BF16),
    relay=pltpu.VMEM((4, 4, 16, WIDE), BF16),
    q1=pltpu.VMEM((4, 4, 16, WIDE), F32),
    sb2=pltpu.VMEM((4, 4, 16, WIDE), BF16),
    rb2=pltpu.VMEM((3, 4, 16, WIDE), BF16),
    q2=pltpu.VMEM((4, 16, WIDE), F32),
    sb3=pltpu.VMEM((4, 16, WIDE), BF16),
    rb3=pltpu.VMEM((3, 16, WIDE), BF16),
    fin=pltpu.VMEM((2, 2, 16, HALF), F32),
    obuf=pltpu.VMEM((2, 4, 4, 4, 16, 256), BF16),
    gno=pltpu.VMEM((4, 4, 32, LAT), F32),
    gns=pltpu.VMEM((4, 4, 32, LAT), BF16),
    gnr=pltpu.VMEM((4, 4, 32, LAT), BF16),
    rim_s=pltpu.VMEM((2, 16, LAT), F32),
    rim_r=pltpu.VMEM((4, 16, LAT), F32),
    gwo=pltpu.VMEM((VARS, 2 * HALF), F32),
    glat=pltpu.VMEM((4, 16, LAT), F32),
    out_sem=DMA((6,)),
    loss_s=pltpu.VMEM((4, 8, 128), F32),
    loss_r=pltpu.VMEM((10, 8, 128), F32),
    ag_ss=DMA((18, 3)),
    ag_rs=DMA((18, 3)),
    rs_ss=DMA((6, 3, 3)),
    rs_rs=DMA((6, 3, 3)),
    ring_ss=DMA((9, 4)),
    ring_rs=DMA((9, 4)),
    oa_ss=DMA((2, 3, 3)),
    oa_rs=DMA((2, 3, 3)),
    fin_ss=DMA((5, 3)),
    fin_rs=DMA((5, 3)),
    n_ss=DMA((4,)),
    n_rs=DMA((4,)),
    gn_ss=DMA((4,)),
    gn_rs=DMA((4,)),
    halo_ss=DMA((3,)),
    halo_rs=DMA((3,)),
    rim_ss=DMA((4,)),
    rim_rs=DMA((4,)),
    f_ss=DMA((2,)),
    f_rs=DMA((2,)),
    g_ss=DMA((3,)),
    g_rs=DMA((3,)),
    oc_ss=DMA,
    oc_rs=DMA,
    l_ss=DMA((10,)),
    l_rs=DMA((10,)),
)


def dot(a, b, dims=((1,), (0,)), precision=None):
    return lax.dot_general(a, b, (dims, ((), ())), precision=precision, preferred_element_type=F32)


class Place:
    def __init__(self):
        m, s = lax.axis_index("member"), lax.axis_index("space")
        self.m, self.s = m, s
        self.xl, self.core = m // 2, m % 2
        self.y, self.z, self.xh = s // 8, (s // 2) % 4, s % 2
        self.x = self.xh * 2 + self.xl
        self.turn = 1 - 2 * self.xh

    def device(self, y, z, x):
        return ((x % 2) * 2 + self.core, (y * 4 + z) * 2 + x // 2)

    def at(self, axis):
        return getattr(self, axis)

    def peer(self, axis, step):
        q = dict(y=self.y, z=self.z, x=self.x)
        q[axis] = (q[axis] + step) % 4
        return self.device(**q)

    def core_peer(self):
        return (self.xl * 2 + 1 - self.core, self.s)

    def pair_peer(self):
        return ((1 - self.xl) * 2 + self.core, self.s)

    def cross_peer(self):
        return ((1 - self.xl) * 2 + 1 - self.core, self.s)


class Copies:
    def __init__(self):
        self.sent = []

    def send(self, src, dst, ss, rs, device):
        copy = pltpu.make_async_remote_copy(
            src_ref=src, dst_ref=dst, send_sem=ss, recv_sem=rs, device_id=device, device_id_type=MESH
        )
        copy.start()
        self.sent.append(copy)
        return copy

    def drain(self):
        for copy in self.sent:
            copy.wait_send()


def arrive(copies):
    for copy in copies:
        copy.wait_recv()


def kernel(lat, eidx, ewt, seed, ntab, w_in, w_out, target, area, loss_o, gl_o, gwi_o, gwo_o, *refs):
    r = dict(zip(SCRATCH, refs))
    wbuf, big, nbuf, n_t, hid, gpre, wo = (r[k] for k in ("wbuf", "big", "nbuf", "n_t", "hid", "gpre", "wo"))
    xhat, rstd, tab, small = r["xhat"], r["rstd"], r["tab"], r["small"]
    me = Place()
    c = Copies()
    col0 = pl.multiple_of(me.core * HALF, 128)

    friends = [me.peer(a, k) for a in "yzx" for k in (1, 2, 3)]
    friends += [me.core_peer(), me.cross_peer()]
    barrier = pltpu.get_barrier_semaphore()
    for d in friends:
        pl.semaphore_signal(barrier, inc=1, device_id=d, device_id_type=MESH)

    wbuf[me.y, me.z, me.x] = w_in[pl.ds(pl.multiple_of(me.xl * 16, 16), 16), pl.ds(col0, HALF)]
    lat32 = [lat[i].astype(F32) for i in range(4)]
    r["halo_s"][0] = jnp.concatenate([v[12:16] for v in lat32], axis=0).astype(BF16)
    r["halo_s"][1] = jnp.concatenate([v[0:4] for v in lat32], axis=0).astype(BF16)
    pl.semaphore_wait(barrier, len(friends))

    halo_s, halo_r = r["halo_s"], r["halo_r"]

    def halo_send(src, dst, k, device):
        return c.send(src, dst, r["halo_ss"].at[k], r["halo_rs"].at[k], device)

    halo = [halo_send(halo_s, halo_r.at[pl.ds(0, 2)], 0, me.peer("x", 2))]

    def gather_send(slot, group, stage, c0, cw):
        order = GROUPS[group][0]
        index = tuple(pl.ds(0, 4) if a in order[:stage] else pl.ds(me.at(a), 1) for a in "yzx")
        index += (slice(None), pl.ds(c0, cw))
        here = wbuf.at[index]
        return [
            c.send(here, here, r["ag_ss"].at[slot, i - 1], r["ag_rs"].at[slot, i - 1], me.peer(order[stage], i))
            for i in (2, 1, 3)
        ]

    gathered = {}

    def gather_stage(stage):
        for g in SEND_ORDER:
            _, c0, cw = GROUPS[g]
            arrive(gathered.pop(g, []))
            gathered[g] = gather_send(6 * stage + g, g, stage, c0, cw)

    gather_stage(0)

    node = lax.broadcasted_iota(jnp.int32, (128, 128), 0)
    row_of = jnp.where(node < 16, node + HALO, jnp.where(node < 20, node - 16, jnp.where(node < 24, node, -1)))
    table_t = jnp.zeros((128, 128), F32)
    for k in range(3):
        table_t = table_t + jnp.where(row_of == eidx[k : k + 1, :], ewt[k : k + 1, :], 0.0)
    tab[...] = table_t
    table = table_t.T[:, :32]
    t_hi = table.astype(BF16)
    t_rest = table - t_hi.astype(F32)
    t_mid = t_rest.astype(BF16)
    t_low = (t_rest - t_mid.astype(F32)).astype(BF16)
    small[0] = jnp.zeros((128, 128), F32)
    small[0, 0:VARS] = target[...]
    small[1] = small[0].T
    small[2] = jnp.broadcast_to(area[...], (128, 128)).T

    arrive(halo)
    halo = [halo_send(halo_r.at[me.xh], halo_r.at[2], 1, me.peer("z", me.turn))]
    gather_stage(1)
    arrive(halo)
    halo = [halo_send(halo_r.at[2], halo_r.at[3], 2, me.peer("y", me.turn))]
    big[0, 0:2, :, :, 0:HALF] = jnp.zeros((2, 4, 16, HALF), F32)
    head = w_out[:, pl.ds(col0, HALF)].astype(F32)
    for v in range(6):
        big[0, v // 4, v % 4, :, 0:HALF] = head[16 * v : 16 * v + 16]
    big[0, 1, 2, 0:4, 0:HALF] = head[96:100]
    wo[...] = big[0, 0:2, :, :, 0:HALF].reshape(128, HALF).astype(BF16)
    r["wo_t"][...] = wo[...].T

    gather_stage(2)

    arrive(halo)
    has_prev = (me.s > 0).astype(F32)
    has_next = (me.s < 31).astype(F32)
    prev_at = jnp.where(me.xh == 0, jnp.where(me.z == 0, 3, 2), 0)
    next_at = jnp.where(me.xh == 1, jnp.where(me.z == 3, 3, 2), 1)
    prev_rows = halo_r[prev_at].astype(F32) * has_prev
    next_rows = halo_r[next_at].astype(F32) * has_next
    normed = []
    for i in range(4):
        edges = [lat[i].astype(F32), prev_rows[4 * i : 4 * i + 4], next_rows[4 * i : 4 * i + 4]]
        window = jnp.concatenate(edges + [jnp.zeros((8, LAT), F32)], axis=0).astype(BF16)
        xhat[i] = dot(t_hi, window) + dot(t_mid, window) + dot(t_low, window)
        scale = 1.0 + ntab[pl.ds(seed[i], 1), :]
        row = me.core * 4 + i

        @pl.loop(0, 4)
        def _(j):
            rows = pl.ds(pl.multiple_of(j * 32, 32), 32)
            a = xhat[i, rows, :]
            centred = a - jnp.mean(a, axis=-1, keepdims=True)
            inv = lax.rsqrt(jnp.mean(centred * centred, axis=-1, keepdims=True) + EPS)
            unit = centred * inv
            xhat[i, rows, :] = unit
            rstd[i, rows, :] = jnp.broadcast_to(inv, (32, 128))
            nbuf[j, row] = (unit * scale).astype(BF16)

        normed.append(c.send(nbuf.at[:, row], nbuf.at[:, row], r["n_ss"].at[i], r["n_rs"].at[i], me.core_peer()))
    arrive(normed)
    for g in range(4):
        n_t[:, 256 * g : 256 * g + 256] = nbuf[g].reshape(256, LAT).T

    fpart, fcore, fsum, fother, gf, gfo = (r[k] for k in ("fpart", "fcore", "fsum", "fother", "gf", "gfo"))
    fpart[...] = jnp.zeros_like(fpart)
    for c0, sources in CHUNKS:
        for g in sources:
            arrive(gathered.pop(g, []))
        cols = slice(c0, c0 + 256)

        w = wbuf[:, :, :, :, cols].reshape(LAT, 256)
        for h in range(4):
            pre = dot(nbuf[h].reshape(256, LAT), w)
            sq = pre * pre
            t = jnp.tanh(pre * (GELU_C + (GELU_C * 0.044715) * sq))
            cdf = 0.5 + 0.5 * t
            act = (pre * cdf).astype(BF16)
            hid[h, :, cols] = act
            slope = cdf + (0.5 * pre) * (1.0 - t * t) * (GELU_C + (3.0 * GELU_C * 0.044715) * sq)
            big[h, :, :, :, cols] = slope.reshape(4, 4, 16, 256)
        for h in range(4):
            fpart[h] += dot(hid[h, :, cols], r["wo_t"][cols, :]).reshape(8, 32, 128)

    f1 = c.send(
        fpart.at[pl.ds(2 * (1 - me.core), 2)], fcore, r["f_ss"].at[0], r["f_rs"].at[0], me.core_peer()
    )
    f1.wait_recv()
    for g in range(2):
        fsum[g] = fpart[2 * me.core + g] + fcore[g]
    f2 = c.send(fsum.at[1 - me.xl], fother, r["f_ss"].at[1], r["f_rs"].at[1], me.pair_peer())
    group = me.core * 2 + me.xl
    f2.wait_recv()

    r["loss_s"][0] = jnp.zeros((8, 128), F32)
    lane = lax.broadcasted_iota(jnp.int32, (8, 128), 1)

    @pl.loop(0, 4)
    def _(j):
        rows = pl.ds(pl.multiple_of(j * 8, 8), 8)
        point = pl.ds(pl.multiple_of(group * 32 + j * 8, 8), 8)
        f = [fsum[me.xl, i, rows, :] for i in range(8)] + [fother[i, rows, :] for i in range(8)]
        weighted = jnp.where(lane < VARS, small[2, point, :] / VARS, 0.0)
        goal = small[1, point, :]
        signs = [jnp.zeros((8, 128), F32) for _ in range(MEMBERS)]
        pairs = jnp.zeros((8, 128), F32)
        for a in range(MEMBERS):
            for b in range(a + 1, MEMBERS):
                d = f[a] - f[b]
                q = d * d + SMOOTH
                inv = lax.rsqrt(q)
                pairs = pairs + q * inv
                sl = d * inv
                signs[a] = signs[a] + sl
                signs[b] = signs[b] - sl
        misfits = jnp.zeros((8, 128), F32)
        for a in range(MEMBERS):
            d = f[a] - goal
            q = d * d + SMOOTH
            inv = lax.rsqrt(q)
            misfits = misfits + q * inv
            grad = (SCALE * weighted) * ((d * inv) * (1.0 / MEMBERS) - PAIR * signs[a])
            r["small_g"][a, rows, :] = grad
        term = misfits * (1.0 / MEMBERS) - PAIR * (pairs + MEMBERS * 0.5 * 0.2)
        r["loss_s"][0] += weighted * term

    for a in range(8):
        gf[group, a] = r["small_g"][a].astype(BF16)
        gfo[a] = r["small_g"][8 + a].astype(BF16)
    gs = [
        c.send(gfo, gf.at[group], r["g_ss"].at[0], r["g_rs"].at[0], me.pair_peer()),
        c.send(gf.at[group], gf.at[group], r["g_ss"].at[1], r["g_rs"].at[1], me.core_peer()),
    ]

    loss_s, loss_r = r["loss_s"], r["loss_r"]
    loss_pending = []

    def loss_send(level):
        if level == 0:
            loss_pending.append(
                [c.send(loss_s.at[0], loss_r.at[0], r["l_ss"].at[0], r["l_rs"].at[0], me.core_peer())]
            )
            return
        axis = "yzx"[level - 1]
        loss_pending.append(
            [
                c.send(
                    loss_s.at[level], loss_r.at[3 * level - 3 + i], r["l_ss"].at[3 * level - 3 + i],
                    r["l_rs"].at[3 * level - 3 + i], me.peer(axis, i),
                )
                for i in (1, 2, 3)
            ]
        )

    def loss_next(level):
        arrive(loss_pending[level])
        if level == 0:
            loss_s[1] = loss_s[0] + loss_r[0]
            return
        v = me.at("yzx"[level - 1])
        base = 3 * level - 3
        own, one, two, three = loss_s[level], loss_r[base + 1], loss_r[base + 2], loss_r[base + 3]
        total = (own + two) + (one + three)
        if level < 3:
            loss_s[level + 1] = total
        else:
            loss_o[...] = total

    loss_send(0)

    def back(h):
        @pl.loop(0, 2)
        def _(j):
            for k in range(4):
                cols = pl.ds(pl.multiple_of(j * 1024 + k * 256, 256), 256)
                slope = big[h, :, :, :, cols].reshape(256, 256)
                gpre[h, :, cols] = (dot(gf[h].reshape(256, 128), wo[:, cols]) * slope).astype(BF16)

    back(group)
    gs[1].wait_recv()
    back((1 - me.core) * 2 + me.xl)
    pair = me.core * 2 + 1 - me.xl
    gs[0].wait_recv()
    gs.append(c.send(gf.at[pair], gf.at[pair], r["g_ss"].at[2], r["g_rs"].at[2], me.core_peer()))
    back(pair)
    gs[2].wait_recv()
    back((1 - me.core) * 2 + 1 - me.xl)
    r["gf_t"][...] = gf[...].reshape(1024, 128).T

    sb1, rb1, q1, sb2, rb2, q2, sb3, rb3, fin, obuf = (
        r[k] for k in ("sb1", "rb1", "q1", "sb2", "rb2", "q2", "sb3", "rb3", "fin", "obuf")
    )
    flight = {}

    def pick(axis, axes, value, cols):
        return tuple(value if a == axis else slice(None) for a in axes) + (slice(None), cols)

    relay = r["relay"]

    def ring_start(k, c0):
        axis = ORDERS[k][0]
        opposite = (me.at(axis) + 2) % 4
        slot = c0 // 256
        flight[c0] = []
        for i in range(2):
            cols = pl.ds(c0 + 128 * i, 128)
            flight[c0].append(
                c.send(
                    sb1.at[pick(axis, "yzx", opposite, cols)], relay.at[:, :, :, cols],
                    r["ring_ss"].at[slot, i], r["ring_rs"].at[slot, i], me.peer(axis, 1 + 2 * i),
                )
            )

    def ring_pass(k, c0):
        axis = ORDERS[k][0]
        spot = "yzx".index(axis)
        slot = c0 // 256
        passed = []
        for i in range(2):
            flight[c0][i].wait_recv()
            there = (me.at(axis) + 1 + 2 * i) % 4
            cols = slice(c0 + 128 * i, c0 + 128 * i + 128)
            for v in range(4):
                index = [v, slice(None)]
                index.insert(spot, there)
                index = tuple(index) + (slice(None), cols)
                sb1[index] = (big[index] + relay[v, :, :, cols].astype(F32)).astype(BF16)
            whole = pl.ds(c0, 256)
            passed.append(
                c.send(
                    sb1.at[pick(axis, "yzx", there, whole)], rb1.at[i, :, :, :, whole],
                    r["ring_ss"].at[slot, 2 + i], r["ring_rs"].at[slot, 2 + i], me.peer(axis, 1 + 2 * i),
                )
            )
        flight[(k, 0)] = flight.get((k, 0), []) + passed

    def scatter_send(k, stage):
        c0, cw = PARTS[k]
        cols, order = pl.ds(c0, cw), ORDERS[k]
        axis = order[stage]
        axes = [a for a in "yzx" if a not in order[:stage]]
        src, dst = ((sb2, rb2), (sb3, rb3))[stage - 1]
        flight[(k, stage)] = []
        for i in (2, 1, 3):
            there = (me.at(axis) + i) % 4
            flight[(k, stage)].append(
                c.send(
                    src.at[pick(axis, axes, there, cols)],
                    dst.at[(i - 1,) + (slice(None),) * (3 - stage) + (cols,)],
                    r["rs_ss"].at[k, stage, i - 1], r["rs_rs"].at[k, stage, i - 1], me.peer(axis, i),
                )
            )

    def scatter_add(k, stage):
        c0, cw = PARTS[k]
        cols, order = slice(c0, c0 + cw), ORDERS[k]
        axis = order[stage]
        axes = [a for a in "yzx" if a not in order[:stage]]
        arrive(flight[(k, stage)])
        own = (big, q1, q2)[stage]
        dst = (rb1, rb2, rb3)[stage]
        where = me.at(axis)
        if stage == 2:
            total = own[where, :, cols]
            for i in range(3):
                total = total + dst[i, :, cols].astype(F32)
            return total
        spot = axes.index(axis)
        keep, send = ((q1, sb2), (q2, sb3))[stage]
        for v in range(4):
            index = [v] + [slice(None)] * (1 - stage)
            index.insert(spot, where)
            total = own[tuple(index) + (slice(None), cols)]
            for i in range(2 + stage):
                total = total + dst[(i, v) + (slice(None),) * (2 - stage) + (cols,)].astype(F32)
            at = (v,) + (slice(None),) * (2 - stage) + (cols,)
            keep[at] = total
            send[at] = total.astype(BF16)

    def advance(k, stage):
        scatter_add(k, stage)
        scatter_send(k, stage + 1)

    finals = {}

    def final_send(k, i, xl, device):
        c0, cw = PARTS[k]
        here = fin.at[xl, me.core, :, pl.ds(c0, cw)]
        return c.send(here, here, r["fin_ss"].at[k, i], r["fin_rs"].at[k, i], device)

    def finish(k):
        c0, cw = PARTS[k]
        fin[me.xl, me.core, :, c0 : c0 + cw] = scatter_add(k, 2) * (1.0 / SCALE)
        finals[k] = [
            final_send(k, 0, me.xl, me.pair_peer()),
            final_send(k, 1, me.xl, me.core_peer()),
        ]

    def finish_pass(k):
        finals[k][0].wait_recv()
        finals[k][0] = final_send(k, 2, 1 - me.xl, me.core_peer())

    out_flight = {}

    def out_stage(part, stage):
        order = ("yzx", "xyz")[part]
        c0 = 128 * part
        if stage == 0:
            if part == 0:
                obuf[me.core, me.y, me.z, me.x] = scatter_add(OUT, 2).astype(BF16)
        else:
            arrive(out_flight[part])
        if stage == 3:
            return
        index = (me.core,)
        index += tuple(pl.ds(0, 4) if a in order[:stage] else pl.ds(me.at(a), 1) for a in "yzx")
        index += (slice(None), pl.ds(c0, 128))
        out_flight[part] = [
            c.send(
                obuf.at[index], obuf.at[index], r["oa_ss"].at[part, stage, i - 1], r["oa_rs"].at[part, stage, i - 1],
                me.peer(order[stage], i),
            )
            for i in (2, 1, 3)
        ]

    @pl.loop(0, 8)
    def _(hg):
        cols = pl.ds(pl.multiple_of(hg * 256, 256), 256)
        part = dot(r["gf_t"][...], hid[:, :, cols].reshape(1024, 256))
        for vg in range(8):
            block = part[16 * vg : 16 * vg + 16]
            y, z, x = vg // 2, (vg % 2) * 2 + hg // 4, hg % 4
            big[y, z, x, :, HALF:WIDE] = block
            sb1[y, z, x, :, HALF:WIDE] = block.astype(BF16)

    ring_start(OUT, HALF)

    def column_part(k, c0):
        cols = slice(c0, c0 + 256)
        for y in range(4):
            rows = slice(256 * y, 256 * y + 256)
            grad = dot(n_t[rows, :], gpre[:, :, cols].reshape(1024, 256)).reshape(4, 4, 16, 256)
            big[y, :, :, :, cols] = grad
            sb1[y, :, :, :, cols] = grad.astype(BF16)
        ring_start(k, c0)

    gno, gns, gnr = r["gno"], r["gns"], r["gnr"]

    def grad_normed(core, dst, n):
        members = pl.ds(pl.multiple_of(core * 128, 128), 128)
        part = dot(gpre[:, members, :].reshape(512, HALF), wbuf[n].reshape(256, HALF), ((1,), (1,)))
        dst[:, :, :, 256 * n : 256 * n + 256] = part.reshape(4, 4, 32, 256).astype(dst.dtype)

    glat, rim_s, rim_r = r["glat"], r["rim_s"], r["rim_r"]

    def norm_back(i):
        scale = 1.0 + ntab[pl.ds(seed[i], 1), :]
        gn[i].wait_recv()
        for j in range(4):
            rows = slice(32 * j, 32 * j + 32)
            g = (gno[j, i] + gnr[j, i].astype(F32)) * scale
            unit = xhat[i, rows, :]
            m1 = jnp.mean(g, axis=-1, keepdims=True)
            m2 = jnp.mean(g * unit, axis=-1, keepdims=True)
            inv = rstd[i, rows, :][:, 0:1]
            xhat[i, rows, :] = inv * (g - m1 - unit * m2)
        rows = dot(tab[0:32, :], xhat[i], precision=lax.Precision.HIGHEST)
        glat[i] = rows[0:16]
        rim_s[0, 4 * i : 4 * i + 4, :] = rows[16:20]
        rim_s[1, 4 * i : 4 * i + 4, :] = rows[20:24]

    def rim_send(src, dst, k, device):
        return c.send(src, dst, r["rim_ss"].at[k], r["rim_rs"].at[k], device)

    column_part(X1, 0)
    column_part(Y1, 256)
    column_part(Z2, 1536)
    column_part(X2, 512)
    column_part(Y2, 1024)
    ring_pass(OUT, HALF)
    column_part(Z2, 1792)
    ring_pass(X1, 0)
    column_part(X2, 768)
    ring_pass(Y1, 256)
    column_part(Y2, 1280)
    ring_pass(Z2, 1536)
    loss_next(0)
    loss_send(1)
    grad_normed(1 - me.core, gns, 0)
    ring_pass(X2, 512)
    grad_normed(1 - me.core, gns, 1)
    ring_pass(Y2, 1024)
    ring_pass(Z2, 1792)
    advance(OUT, 0)
    grad_normed(1 - me.core, gns, 2)
    ring_pass(X2, 768)
    grad_normed(1 - me.core, gns, 3)
    gn = [c.send(gns.at[:, i], gnr.at[:, i], r["gn_ss"].at[i], r["gn_rs"].at[i], me.core_peer()) for i in range(4)]
    ring_pass(Y2, 1280)
    for k in (X1, Y1):
        advance(k, 0)
    loss_next(1)
    loss_send(2)
    for n in range(4):
        grad_normed(me.core, gno, n)
    advance(OUT, 1)
    norm_back(0)
    norm_back(1)
    for k in (X1, Y1):
        advance(k, 1)
    for k in (Z2, X2, Y2):
        advance(k, 0)
    out_stage(0, 0)
    out_stage(1, 0)
    loss_next(2)
    loss_send(3)
    norm_back(2)
    norm_back(3)
    near = rim_send(rim_s.at[1 - me.xh], rim_r.at[0], 0, me.peer("x", 2))
    far = rim_send(rim_s.at[me.xh], rim_r.at[1], 1, me.peer("z", -me.turn))
    finish(X1)
    finish(Y1)
    out_stage(0, 1)
    out_stage(1, 1)
    for k in (Z2, X2, Y2):
        advance(k, 1)
    far.wait_recv()
    far = rim_send(rim_r.at[1], rim_r.at[2], 2, me.peer("y", -me.turn))
    for k in (X1, Y1):
        finish_pass(k)
    out_stage(0, 2)
    out_stage(1, 2)
    far.wait_recv()
    carried = jnp.where(me.xh == 0, me.z == 3, me.z == 0)
    last = rim_send(rim_r.at[jnp.where(carried, 2, 1)], rim_r.at[3], 3, me.peer("x", 2))
    for k in (Z2, X2, Y2):
        finish(k)
    loss_next(3)
    out_stage(0, 3)
    out_stage(1, 3)
    own_out = obuf.at[me.core]
    oc = c.send(own_out, own_out, r["oc_ss"], r["oc_rs"], me.core_peer())
    near.wait_recv()
    last.wait_recv()
    from_next = rim_r[jnp.where(me.xh == 0, 0, 3)] * has_next
    from_prev = rim_r[jnp.where(me.xh == 0, 3, 0)] * has_prev
    for i in range(4):
        glat[i, 12:16, :] += from_next[4 * i : 4 * i + 4]
        glat[i, 0:4, :] += from_prev[4 * i : 4 * i + 4]
    leave = [pltpu.make_async_copy(glat, gl_o, r["out_sem"].at[0])]
    leave[0].start()
    for k in (Z2, X2, Y2):
        finish_pass(k)
    oc.wait_recv()
    gwo = r["gwo"]
    for core in range(2):
        for b in range(56):
            vg, hg = b // 8, b % 8
            rows = min(16, VARS - 16 * vg)
            block = obuf[core, b // 16, (b // 4) % 4, b % 4].astype(F32) * (1.0 / SCALE)
            at = core * HALF + 256 * hg
            gwo[16 * vg : 16 * vg + rows, at : at + 256] = block[0:rows]
    leave.append(pltpu.make_async_copy(gwo, gwo_o, r["out_sem"].at[1]))
    leave[1].start()
    for k in finals:
        arrive(finals[k])
    for xl in range(2):
        for core in range(2):
            dst = gwi_o.at[pl.ds(16 * xl, 16), pl.ds(HALF * core, HALF)]
            leave.append(pltpu.make_async_copy(fin.at[xl, core], dst, r["out_sem"].at[2 + 2 * xl + core]))
            leave[-1].start()
    for copy in leave:
        copy.wait()
    c.drain()


SCRATCH["small_g"] = pltpu.VMEM((16, 32, 128), F32)


def hand_on(loss, gl, gwi, gwo, loss_o, gl_o, gwi_o, gwo_o):
    loss_o[0, 0] = jnp.sum(loss[...]) * (1.0 / POINTS)
    gl_o[...] = gl[...]
    gwi_o[...] = gwi[...]
    gwo_o[...] = gwo[...]


def local(latent, edge_index, edge_weight, noise_seed, noise_table, w_in, w_out, target, area_weight):
    vmem = pl.BlockSpec(memory_space=pltpu.VMEM)
    smem = pl.BlockSpec(memory_space=pltpu.SMEM)
    anywhere = pl.BlockSpec(memory_space=pl.ANY)
    grads = (
        jax.ShapeDtypeStruct((4, 16, LAT), F32),
        jax.ShapeDtypeStruct((32, 2 * HALF), F32),
        jax.ShapeDtypeStruct((VARS, 2 * HALF), F32),
    )
    made = pl.pallas_call(
        kernel,
        out_shape=(jax.ShapeDtypeStruct((8, 128), F32),) + grads,
        in_specs=[vmem, vmem, vmem, smem] + [vmem] * 5,
        out_specs=(vmem,) + (anywhere,) * 3,
        scratch_shapes=list(SCRATCH.values()),
        compiler_params=pltpu.CompilerParams(
            collective_id=0, has_side_effects=True, vmem_limit_bytes=63 * 2**20
        ),
    )(latent, edge_index, edge_weight, noise_seed, noise_table, w_in, w_out, target, area_weight.reshape(1, -1))
    loss, grad_latent, grad_in, grad_out = pl.pallas_call(
        hand_on,
        out_shape=(jax.ShapeDtypeStruct((1, 1), F32),) + grads,
        in_specs=[vmem] * 4,
        out_specs=(smem,) + (vmem,) * 3,
    )(*made)
    return (loss[0, 0], grad_latent, grad_in, grad_out)


def solution(mesh):
    return jax.shard_map(
        local,
        mesh=mesh,
        in_specs=(
            P("member", "space", None),
            P(None, "space"),
            P(None, "space"),
            P("member"),
            P(),
            P("space", None),
            P(),
            P(None, "space"),
            P("space"),
        ),
        out_specs=(P(), P("member", "space", None), P("space", None), P()),
        check_vma=False,
    )
```

```python
import jax
import jax.numpy as jnp
from jax import lax
from jax.experimental import pallas as pl
from jax.experimental.pallas import tpu as pltpu
from jax.sharding import PartitionSpec as P

VARS = 100
HALO = 4
MEMBERS = 16
POINTS = 4096
F32 = jnp.float32
BF16 = jnp.bfloat16
EPS = 1e-05
SMOOTH = 0.04
SCALE = 1024.0
PAIR = 1.0 / (MEMBERS * (MEMBERS - 1))
GELU_C = 0.7978845608028654
MESH = pl.DeviceIdType.MESH

LAT = 1024
HALF = 2048
WIDE = HALF + 256
GROUPS = [
    ("yzx", 0, 384),
    ("zyx", 384, 384),
    ("xzy", 768, 384),
    ("zxy", 1152, 384),
    ("xyz", 1536, 256),
    ("yxz", 1792, 256),
]
SEND_ORDER = (0, 2, 4, 1, 3, 5)
CHUNKS = [(0, (0,)), (768, (2,)), (1536, (4,)), (256, (0, 1)), (512, (1,)), (1024, (2, 3)), (1280, (3,)), (1792, (5,))]
PARTS = [(0, 256), (256, 256), (1536, 512), (512, 512), (1024, 512), (2048, 256)]
ORDERS = ["xyz", "yzx", "zyx", "xzy", "yxz", "zxy"]
X1, Y1, Z2, X2, Y2, OUT = range(6)

DMA = pltpu.SemaphoreType.DMA
SCRATCH = dict(
    wbuf=pltpu.VMEM((4, 4, 4, 16, HALF), BF16),
    wo=pltpu.VMEM((128, HALF), BF16),
    wo_t=pltpu.VMEM((HALF, 128), BF16),
    nbuf=pltpu.VMEM((4, 8, 32, LAT), BF16),
    n_t=pltpu.VMEM((LAT, 1024), BF16),
    xhat=pltpu.VMEM((4, 128, LAT), F32),
    rstd=pltpu.VMEM((4, 128, 128), F32),
    tab=pltpu.VMEM((128, 128), F32),
    small=pltpu.VMEM((3, 128, 128), F32),
    hid=pltpu.VMEM((4, 256, HALF), BF16),
    big=pltpu.VMEM((4, 4, 4, 16, WIDE), F32),
    gpre=pltpu.VMEM((4, 256, HALF), BF16),
    halo_s=pltpu.VMEM((2, 16, LAT), BF16),
    halo_r=pltpu.VMEM((4, 16, LAT), BF16),
    fpart=pltpu.VMEM((4, 8, 32, 128), F32),
    fcore=pltpu.VMEM((2, 8, 32, 128), F32),
    fsum=pltpu.VMEM((2, 8, 32, 128), F32),
    fother=pltpu.VMEM((8, 32, 128), F32),
    gf=pltpu.VMEM((4, 8, 32, 128), BF16),
    gfo=pltpu.VMEM((8, 32, 128), BF16),
    gf_t=pltpu.VMEM((128, 1024), BF16),
    sb1=pltpu.VMEM((4, 4, 4, 16, WIDE), BF16),
    rb1=pltpu.VMEM((2, 4, 4, 16, WIDE), BF16),
    relay=pltpu.VMEM((4, 4, 16, WIDE), BF16),
    q1=pltpu.VMEM((4, 4, 16, WIDE), F32),
    sb2=pltpu.VMEM((4, 4, 16, WIDE), BF16),
    rb2=pltpu.VMEM((3, 4, 16, WIDE), BF16),
    q2=pltpu.VMEM((4, 16, WIDE), F32),
    sb3=pltpu.VMEM((4, 16, WIDE), BF16),
    rb3=pltpu.VMEM((3, 16, WIDE), BF16),
    fin=pltpu.VMEM((2, 2, 16, HALF), F32),
    obuf=pltpu.VMEM((2, 4, 4, 4, 16, 256), BF16),
    gno=pltpu.VMEM((4, 4, 32, LAT), F32),
    gns=pltpu.VMEM((4, 4, 32, LAT), BF16),
    gnr=pltpu.VMEM((4, 4, 32, LAT), BF16),
    rim_s=pltpu.VMEM((2, 16, LAT), F32),
    rim_r=pltpu.VMEM((4, 16, LAT), F32),
    glat=pltpu.VMEM((4, 16, LAT), F32),
    out_sem=DMA((6,)),
    loss_s=pltpu.VMEM((4, 8, 128), F32),
    loss_r=pltpu.VMEM((10, 8, 128), F32),
    ag_ss=DMA((18, 3)),
    ag_rs=DMA((18, 3)),
    rs_ss=DMA((6, 3, 3)),
    rs_rs=DMA((6, 3, 3)),
    ring_ss=DMA((9, 4)),
    ring_rs=DMA((9, 4)),
    oa_ss=DMA((2, 3, 3)),
    oa_rs=DMA((2, 3, 3)),
    fin_ss=DMA((5, 3)),
    fin_rs=DMA((5, 3)),
    n_ss=DMA((4,)),
    n_rs=DMA((4,)),
    gn_ss=DMA((4,)),
    gn_rs=DMA((4,)),
    halo_ss=DMA((3,)),
    halo_rs=DMA((3,)),
    rim_ss=DMA((4,)),
    rim_rs=DMA((4,)),
    f_ss=DMA((2,)),
    f_rs=DMA((2,)),
    g_ss=DMA((3,)),
    g_rs=DMA((3,)),
    oc_ss=DMA,
    oc_rs=DMA,
    l_ss=DMA((10,)),
    l_rs=DMA((10,)),
)


def dot(a, b, dims=((1,), (0,)), precision=None):
    return lax.dot_general(a, b, (dims, ((), ())), precision=precision, preferred_element_type=F32)


class Place:
    def __init__(self):
        m, s = lax.axis_index("member"), lax.axis_index("space")
        self.m, self.s = m, s
        self.xl, self.core = lax.div(m, 2), lax.rem(m, 2)
        self.y, self.z, self.xh = lax.div(s, 8), lax.rem(lax.div(s, 2), 4), lax.rem(s, 2)
        self.x = self.xh * 2 + self.xl
        self.turn = 1 - 2 * self.xh
        self.steps = {(a, 0): getattr(self, a) for a in "yzx"}
        self.peers = {}
        for a in "yzx":
            for k in (1, 2, 3):
                self.steps[a, k] = lax.rem(self.steps[a, 0] + k, 4)
                self.peers[a, k] = self.device(**{b: self.steps[b, k if a == b else 0] for b in "yzx"})

    def device(self, y, z, x):
        return (lax.rem(x, 2) * 2 + self.core, (y * 4 + z) * 2 + lax.div(x, 2))

    def at(self, axis, step=0):
        return self.steps[axis, step]

    def peer(self, axis, step):
        if isinstance(step, int):
            return self.peers[axis, step]
        q = dict(y=self.y, z=self.z, x=self.x)
        q[axis] = lax.rem(q[axis] + step + 4, 4)
        return self.device(**q)

    def core_peer(self):
        return (self.xl * 2 + 1 - self.core, self.s)

    def pair_peer(self):
        return ((1 - self.xl) * 2 + self.core, self.s)


class Copies:
    def __init__(self):
        self.sent = []

    def send(self, src, dst, ss, rs, device):
        copy = pltpu.make_async_remote_copy(
            src_ref=src, dst_ref=dst, send_sem=ss, recv_sem=rs, device_id=device, device_id_type=MESH
        )
        copy.start()
        self.sent.append(copy)
        return copy

    def drain(self):
        for copy in self.sent:
            copy.wait_send()


def arrive(copies):
    for copy in copies:
        copy.wait_recv()


def kernel(lat, eidx, ewt, seed, ntab, w_in, w_out, target, area, loss_o, gl_o, gwi_o, gwo_o, *refs):
    r = dict(zip(SCRATCH, refs))
    wbuf, big, nbuf, n_t, hid, gpre, wo = (r[k] for k in ("wbuf", "big", "nbuf", "n_t", "hid", "gpre", "wo"))
    xhat, rstd, tab, small = r["xhat"], r["rstd"], r["tab"], r["small"]
    me = Place()
    c = Copies()
    col0 = pl.multiple_of(me.core * HALF, 128)

    friends = [me.peer(a, k) for a in "yzx" for k in (1, 2, 3)]
    friends.append(me.core_peer())
    barrier = pltpu.get_barrier_semaphore()
    for d in friends:
        pl.semaphore_signal(barrier, inc=1, device_id=d, device_id_type=MESH)

    wbuf[me.y, me.z, me.x] = w_in[pl.ds(pl.multiple_of(me.xl * 16, 16), 16), pl.ds(col0, HALF)]
    lat32 = [lat[i].astype(F32) for i in range(4)]
    r["halo_s"][0] = jnp.concatenate([v[12:16] for v in lat32], axis=0).astype(BF16)
    r["halo_s"][1] = jnp.concatenate([v[0:4] for v in lat32], axis=0).astype(BF16)
    pl.semaphore_wait(barrier, len(friends))

    halo_s, halo_r = r["halo_s"], r["halo_r"]

    def halo_send(src, dst, k, device):
        return c.send(src, dst, r["halo_ss"].at[k], r["halo_rs"].at[k], device)

    halo = [halo_send(halo_s, halo_r.at[pl.ds(0, 2)], 0, me.peer("x", 2))]

    def gather_send(slot, group, stage, c0, cw):
        order = GROUPS[group][0]
        index = tuple(pl.ds(0, 4) if a in order[:stage] else pl.ds(me.at(a), 1) for a in "yzx")
        index += (slice(None), pl.ds(c0, cw))
        here = wbuf.at[index]
        return [
            c.send(here, here, r["ag_ss"].at[slot, i - 1], r["ag_rs"].at[slot, i - 1], me.peer(order[stage], i))
            for i in (2, 1, 3)
        ]

    gathered = {}

    def gather_stage(stage):
        for g in SEND_ORDER:
            _, c0, cw = GROUPS[g]
            arrive(gathered.pop(g, []))
            gathered[g] = gather_send(6 * stage + g, g, stage, c0, cw)

    gather_stage(0)

    node = lax.broadcasted_iota(jnp.int32, (128, 128), 0)
    row_of = jnp.where(node < 16, node + HALO, jnp.where(node < 20, node - 16, jnp.where(node < 24, node, -1)))
    table_t = jnp.zeros((128, 128), F32)
    for k in range(3):
        table_t = table_t + jnp.where(row_of == eidx[k : k + 1, :], ewt[k : k + 1, :], 0.0)
    tab[...] = table_t
    table = table_t.T[:, :32]
    t_hi = table.astype(BF16)
    t_rest = table - t_hi.astype(F32)
    t_mid = t_rest.astype(BF16)
    t_low = (t_rest - t_mid.astype(F32)).astype(BF16)
    small[0] = jnp.zeros((128, 128), F32)
    small[0, 0:VARS] = target[...]
    small[1] = small[0].T
    small[2] = jnp.broadcast_to(area[...], (128, 128)).T

    arrive(halo)
    halo = [halo_send(halo_r.at[me.xh], halo_r.at[2], 1, me.peer("z", me.turn))]
    gather_stage(1)
    arrive(halo)
    halo = [halo_send(halo_r.at[2], halo_r.at[3], 2, me.peer("y", me.turn))]
    big[0, 0:2, :, :, 0:HALF] = jnp.zeros((2, 4, 16, HALF), F32)
    head = w_out[:, pl.ds(col0, HALF)].astype(F32)
    for v in range(6):
        big[0, v // 4, v % 4, :, 0:HALF] = head[16 * v : 16 * v + 16]
    big[0, 1, 2, 0:4, 0:HALF] = head[96:100]
    wo[...] = big[0, 0:2, :, :, 0:HALF].reshape(128, HALF).astype(BF16)
    r["wo_t"][...] = wo[...].T

    gather_stage(2)

    arrive(halo)
    has_prev = (me.s > 0).astype(F32)
    has_next = (me.s < 31).astype(F32)
    prev_at = jnp.where(me.xh == 0, jnp.where(me.z == 0, 3, 2), 0)
    next_at = jnp.where(me.xh == 1, jnp.where(me.z == 3, 3, 2), 1)
    prev_rows = halo_r[prev_at].astype(F32) * has_prev
    next_rows = halo_r[next_at].astype(F32) * has_next
    normed = []
    for i in range(4):
        edges = [lat[i].astype(F32), prev_rows[4 * i : 4 * i + 4], next_rows[4 * i : 4 * i + 4]]
        window = jnp.concatenate(edges + [jnp.zeros((8, LAT), F32)], axis=0).astype(BF16)
        xhat[i] = dot(t_hi, window) + dot(t_mid, window) + dot(t_low, window)
        scale = 1.0 + ntab[pl.ds(seed[i], 1), :]
        row = me.core * 4 + i

        @pl.loop(0, 4)
        def _(j):
            rows = pl.ds(pl.multiple_of(j * 32, 32), 32)
            a = xhat[i, rows, :]
            centred = a - jnp.mean(a, axis=-1, keepdims=True)
            inv = lax.rsqrt(jnp.mean(centred * centred, axis=-1, keepdims=True) + EPS)
            unit = centred * inv
            xhat[i, rows, :] = unit
            rstd[i, rows, :] = jnp.broadcast_to(inv, (32, 128))
            nbuf[j, row] = (unit * scale).astype(BF16)

        normed.append(c.send(nbuf.at[:, row], nbuf.at[:, row], r["n_ss"].at[i], r["n_rs"].at[i], me.core_peer()))
    arrive(normed)
    for g in range(4):
        n_t[:, 256 * g : 256 * g + 256] = nbuf[g].reshape(256, LAT).T

    fpart, fcore, fsum, fother, gf, gfo = (r[k] for k in ("fpart", "fcore", "fsum", "fother", "gf", "gfo"))
    fpart[...] = jnp.zeros_like(fpart)
    for c0, sources in CHUNKS:
        for g in sources:
            arrive(gathered.pop(g, []))
        cols = slice(c0, c0 + 256)

        w = wbuf[:, :, :, :, cols].reshape(LAT, 256)
        for h in range(4):
            pre = dot(nbuf[h].reshape(256, LAT), w)
            sq = pre * pre
            t = jnp.tanh(pre * (GELU_C + (GELU_C * 0.044715) * sq))
            cdf = 0.5 + 0.5 * t
            act = (pre * cdf).astype(BF16)
            hid[h, :, cols] = act
            slope = cdf + (0.5 * pre) * (1.0 - t * t) * (GELU_C + (3.0 * GELU_C * 0.044715) * sq)
            big[h, :, :, :, cols] = slope.reshape(4, 4, 16, 256)
        for h in range(4):
            fpart[h] += dot(hid[h, :, cols], r["wo_t"][cols, :]).reshape(8, 32, 128)

    f1 = c.send(
        fpart.at[pl.ds(2 * (1 - me.core), 2)], fcore, r["f_ss"].at[0], r["f_rs"].at[0], me.core_peer()
    )
    f1.wait_recv()
    for g in range(2):
        fsum[g] = fpart[2 * me.core + g] + fcore[g]
    f2 = c.send(fsum.at[1 - me.xl], fother, r["f_ss"].at[1], r["f_rs"].at[1], me.pair_peer())
    group = me.core * 2 + me.xl
    f2.wait_recv()

    r["loss_s"][0] = jnp.zeros((8, 128), F32)
    lane = lax.broadcasted_iota(jnp.int32, (8, 128), 1)

    @pl.loop(0, 4)
    def _(j):
        rows = pl.ds(pl.multiple_of(j * 8, 8), 8)
        point = pl.ds(pl.multiple_of(group * 32 + j * 8, 8), 8)
        f = [fsum[me.xl, i, rows, :] for i in range(8)] + [fother[i, rows, :] for i in range(8)]
        weighted = jnp.where(lane < VARS, small[2, point, :] / VARS, 0.0)
        goal = small[1, point, :]
        signs = [jnp.zeros((8, 128), F32) for _ in range(MEMBERS)]
        pairs = jnp.zeros((8, 128), F32)
        for a in range(MEMBERS):
            for b in range(a + 1, MEMBERS):
                d = f[a] - f[b]
                q = d * d + SMOOTH
                inv = lax.rsqrt(q)
                pairs = pairs + q * inv
                sl = d * inv
                signs[a] = signs[a] + sl
                signs[b] = signs[b] - sl
        misfits = jnp.zeros((8, 128), F32)
        for a in range(MEMBERS):
            d = f[a] - goal
            q = d * d + SMOOTH
            inv = lax.rsqrt(q)
            misfits = misfits + q * inv
            grad = (SCALE * weighted) * ((d * inv) * (1.0 / MEMBERS) - PAIR * signs[a])
            r["small_g"][a, rows, :] = grad
        term = misfits * (1.0 / MEMBERS) - PAIR * (pairs + MEMBERS * 0.5 * 0.2)
        r["loss_s"][0] += weighted * term

    for a in range(8):
        gf[group, a] = r["small_g"][a].astype(BF16)
        gfo[a] = r["small_g"][8 + a].astype(BF16)
    gs = [
        c.send(gfo, gf.at[group], r["g_ss"].at[0], r["g_rs"].at[0], me.pair_peer()),
        c.send(gf.at[group], gf.at[group], r["g_ss"].at[1], r["g_rs"].at[1], me.core_peer()),
    ]

    loss_s, loss_r = r["loss_s"], r["loss_r"]
    loss_pending = []

    def loss_send(level):
        if level == 0:
            loss_pending.append(
                [c.send(loss_s.at[0], loss_r.at[0], r["l_ss"].at[0], r["l_rs"].at[0], me.core_peer())]
            )
            return
        axis = "yzx"[level - 1]
        loss_pending.append(
            [
                c.send(
                    loss_s.at[level], loss_r.at[3 * level - 3 + i], r["l_ss"].at[3 * level - 3 + i],
                    r["l_rs"].at[3 * level - 3 + i], me.peer(axis, i),
                )
                for i in (1, 2, 3)
            ]
        )

    def loss_next(level):
        arrive(loss_pending[level])
        if level == 0:
            loss_s[1] = loss_s[0] + loss_r[0]
            return
        v = me.at("yzx"[level - 1])
        base = 3 * level - 3
        own, one, two, three = loss_s[level], loss_r[base + 1], loss_r[base + 2], loss_r[base + 3]
        total = (own + two) + (one + three)
        if level < 3:
            loss_s[level + 1] = total
        else:
            loss_o[...] = total

    loss_send(0)

    def back(h):
        @pl.loop(0, 2)
        def _(j):
            for k in range(4):
                cols = pl.ds(pl.multiple_of(j * 1024 + k * 256, 256), 256)
                slope = big[h, :, :, :, cols].reshape(256, 256)
                gpre[h, :, cols] = (dot(gf[h].reshape(256, 128), wo[:, cols]) * slope).astype(BF16)

    back(group)
    gs[1].wait_recv()
    back((1 - me.core) * 2 + me.xl)
    pair = me.core * 2 + 1 - me.xl
    gs[0].wait_recv()
    gs.append(c.send(gf.at[pair], gf.at[pair], r["g_ss"].at[2], r["g_rs"].at[2], me.core_peer()))
    back(pair)
    gs[2].wait_recv()
    back((1 - me.core) * 2 + 1 - me.xl)
    r["gf_t"][...] = gf[...].reshape(1024, 128).T

    sb1, rb1, q1, sb2, rb2, q2, sb3, rb3, fin, obuf = (
        r[k] for k in ("sb1", "rb1", "q1", "sb2", "rb2", "q2", "sb3", "rb3", "fin", "obuf")
    )
    flight = {}

    def pick(axis, axes, value, cols):
        return tuple(value if a == axis else slice(None) for a in axes) + (slice(None), cols)

    relay = r["relay"]

    def ring_start(k, c0):
        axis = ORDERS[k][0]
        opposite = me.at(axis, 2)
        slot = c0 // 256
        flight[c0] = []
        for i in range(2):
            cols = pl.ds(c0 + 128 * i, 128)
            flight[c0].append(
                c.send(
                    sb1.at[pick(axis, "yzx", opposite, cols)], relay.at[:, :, :, cols],
                    r["ring_ss"].at[slot, i], r["ring_rs"].at[slot, i], me.peer(axis, 1 + 2 * i),
                )
            )

    def ring_pass(k, c0):
        axis = ORDERS[k][0]
        spot = "yzx".index(axis)
        slot = c0 // 256
        passed = []
        for i in range(2):
            flight[c0][i].wait_recv()
            there = me.at(axis, 1 + 2 * i)
            cols = slice(c0 + 128 * i, c0 + 128 * i + 128)
            for v in range(4):
                index = [v, slice(None)]
                index.insert(spot, there)
                index = tuple(index) + (slice(None), cols)
                sb1[index] = (big[index] + relay[v, :, :, cols].astype(F32)).astype(BF16)
            whole = pl.ds(c0, 256)
            passed.append(
                c.send(
                    sb1.at[pick(axis, "yzx", there, whole)], rb1.at[i, :, :, :, whole],
                    r["ring_ss"].at[slot, 2 + i], r["ring_rs"].at[slot, 2 + i], me.peer(axis, 1 + 2 * i),
                )
            )
        flight[(k, 0)] = flight.get((k, 0), []) + passed

    def scatter_send(k, stage):
        c0, cw = PARTS[k]
        cols, order = pl.ds(c0, cw), ORDERS[k]
        axis = order[stage]
        axes = [a for a in "yzx" if a not in order[:stage]]
        src, dst = ((sb2, rb2), (sb3, rb3))[stage - 1]
        flight[(k, stage)] = []
        for i in (2, 1, 3):
            there = me.at(axis, i)
            flight[(k, stage)].append(
                c.send(
                    src.at[pick(axis, axes, there, cols)],
                    dst.at[(i - 1,) + (slice(None),) * (3 - stage) + (cols,)],
                    r["rs_ss"].at[k, stage, i - 1], r["rs_rs"].at[k, stage, i - 1], me.peer(axis, i),
                )
            )

    def scatter_add(k, stage):
        c0, cw = PARTS[k]
        cols, order = slice(c0, c0 + cw), ORDERS[k]
        axis = order[stage]
        axes = [a for a in "yzx" if a not in order[:stage]]
        arrive(flight[(k, stage)])
        own = (big, q1, q2)[stage]
        dst = (rb1, rb2, rb3)[stage]
        where = me.at(axis)
        if stage == 2:
            total = own[where, :, cols]
            for i in range(3):
                total = total + dst[i, :, cols].astype(F32)
            return total
        spot = axes.index(axis)
        keep, send = ((q1, sb2), (q2, sb3))[stage]
        for v in range(4):
            index = [v] + [slice(None)] * (1 - stage)
            index.insert(spot, where)
            total = own[tuple(index) + (slice(None), cols)]
            for i in range(2 + stage):
                total = total + dst[(i, v) + (slice(None),) * (2 - stage) + (cols,)].astype(F32)
            at = (v,) + (slice(None),) * (2 - stage) + (cols,)
            keep[at] = total
            send[at] = total.astype(BF16)

    def advance(k, stage):
        scatter_add(k, stage)
        scatter_send(k, stage + 1)

    finals = {}

    def final_send(k, i, xl, device):
        c0, cw = PARTS[k]
        here = fin.at[xl, me.core, :, pl.ds(c0, cw)]
        return c.send(here, here, r["fin_ss"].at[k, i], r["fin_rs"].at[k, i], device)

    def finish(k):
        c0, cw = PARTS[k]
        fin[me.xl, me.core, :, c0 : c0 + cw] = scatter_add(k, 2) * (1.0 / SCALE)
        finals[k] = [
            final_send(k, 0, me.xl, me.pair_peer()),
            final_send(k, 1, me.xl, me.core_peer()),
        ]

    def finish_pass(k):
        finals[k][0].wait_recv()
        finals[k][0] = final_send(k, 2, 1 - me.xl, me.core_peer())

    out_flight = {}

    def out_stage(part, stage):
        order = ("yzx", "xyz")[part]
        c0 = 128 * part
        if stage == 0:
            if part == 0:
                obuf[me.core, me.y, me.z, me.x] = scatter_add(OUT, 2).astype(BF16)
        else:
            arrive(out_flight[part])
        if stage == 3:
            return
        index = (me.core,)
        index += tuple(pl.ds(0, 4) if a in order[:stage] else pl.ds(me.at(a), 1) for a in "yzx")
        index += (slice(None), pl.ds(c0, 128))
        out_flight[part] = [
            c.send(
                obuf.at[index], obuf.at[index], r["oa_ss"].at[part, stage, i - 1], r["oa_rs"].at[part, stage, i - 1],
                me.peer(order[stage], i),
            )
            for i in (2, 1, 3)
        ]

    @pl.loop(0, 8)
    def _(hg):
        cols = pl.ds(pl.multiple_of(hg * 256, 256), 256)
        part = dot(r["gf_t"][...], hid[:, :, cols].reshape(1024, 256))
        for vg in range(8):
            block = part[16 * vg : 16 * vg + 16]
            y, z, x = vg // 2, (vg % 2) * 2 + hg // 4, hg % 4
            big[y, z, x, :, HALF:WIDE] = block
            sb1[y, z, x, :, HALF:WIDE] = block.astype(BF16)

    ring_start(OUT, HALF)

    def column_part(k, c0):
        cols = slice(c0, c0 + 256)
        for y in range(4):
            rows = slice(256 * y, 256 * y + 256)
            grad = dot(n_t[rows, :], gpre[:, :, cols].reshape(1024, 256)).reshape(4, 4, 16, 256)
            big[y, :, :, :, cols] = grad
            sb1[y, :, :, :, cols] = grad.astype(BF16)
        ring_start(k, c0)

    gno, gns, gnr = r["gno"], r["gns"], r["gnr"]

    def grad_normed(core, dst, n):
        members = pl.ds(pl.multiple_of(core * 128, 128), 128)
        part = dot(gpre[:, members, :].reshape(512, HALF), wbuf[n].reshape(256, HALF), ((1,), (1,)))
        dst[:, :, :, 256 * n : 256 * n + 256] = part.reshape(4, 4, 32, 256).astype(dst.dtype)

    glat, rim_s, rim_r = r["glat"], r["rim_s"], r["rim_r"]

    def norm_back(i):
        scale = 1.0 + ntab[pl.ds(seed[i], 1), :]
        gn[i].wait_recv()
        for j in range(4):
            rows = slice(32 * j, 32 * j + 32)
            g = (gno[j, i] + gnr[j, i].astype(F32)) * scale
            unit = xhat[i, rows, :]
            m1 = jnp.mean(g, axis=-1, keepdims=True)
            m2 = jnp.mean(g * unit, axis=-1, keepdims=True)
            inv = rstd[i, rows, :][:, 0:1]
            xhat[i, rows, :] = inv * (g - m1 - unit * m2)
        rows = dot(tab[0:32, :], xhat[i], precision=lax.Precision.HIGHEST)
        glat[i] = rows[0:16]
        rim_s[0, 4 * i : 4 * i + 4, :] = rows[16:20]
        rim_s[1, 4 * i : 4 * i + 4, :] = rows[20:24]

    def rim_send(src, dst, k, device):
        return c.send(src, dst, r["rim_ss"].at[k], r["rim_rs"].at[k], device)

    column_part(X1, 0)
    column_part(Y1, 256)
    column_part(Z2, 1536)
    column_part(X2, 512)
    column_part(Y2, 1024)
    ring_pass(OUT, HALF)
    column_part(Z2, 1792)
    ring_pass(X1, 0)
    column_part(X2, 768)
    ring_pass(Y1, 256)
    column_part(Y2, 1280)
    ring_pass(Z2, 1536)
    loss_next(0)
    loss_send(1)
    grad_normed(1 - me.core, gns, 0)
    ring_pass(X2, 512)
    grad_normed(1 - me.core, gns, 1)
    ring_pass(Y2, 1024)
    ring_pass(Z2, 1792)
    advance(OUT, 0)
    grad_normed(1 - me.core, gns, 2)
    ring_pass(X2, 768)
    grad_normed(1 - me.core, gns, 3)
    gn = [c.send(gns.at[:, i], gnr.at[:, i], r["gn_ss"].at[i], r["gn_rs"].at[i], me.core_peer()) for i in range(4)]
    ring_pass(Y2, 1280)
    for k in (X1, Y1):
        advance(k, 0)
    loss_next(1)
    loss_send(2)
    for n in range(4):
        grad_normed(me.core, gno, n)
    advance(OUT, 1)
    norm_back(0)
    norm_back(1)
    for k in (X1, Y1):
        advance(k, 1)
    for k in (Z2, X2, Y2):
        advance(k, 0)
    out_stage(0, 0)
    out_stage(1, 0)
    loss_next(2)
    loss_send(3)
    norm_back(2)
    norm_back(3)
    near = rim_send(rim_s.at[1 - me.xh], rim_r.at[0], 0, me.peer("x", 2))
    far = rim_send(rim_s.at[me.xh], rim_r.at[1], 1, me.peer("z", -me.turn))
    finish(X1)
    finish(Y1)
    out_stage(0, 1)
    out_stage(1, 1)
    for k in (Z2, X2, Y2):
        advance(k, 1)
    far.wait_recv()
    far = rim_send(rim_r.at[1], rim_r.at[2], 2, me.peer("y", -me.turn))
    for k in (X1, Y1):
        finish_pass(k)
    out_stage(0, 2)
    out_stage(1, 2)
    far.wait_recv()
    carried = jnp.where(me.xh == 0, me.z == 3, me.z == 0)
    last = rim_send(rim_r.at[jnp.where(carried, 2, 1)], rim_r.at[3], 3, me.peer("x", 2))
    for k in (Z2, X2, Y2):
        finish(k)
    loss_next(3)
    out_stage(0, 3)
    out_stage(1, 3)
    own_out = obuf.at[me.core]
    oc = c.send(own_out, own_out, r["oc_ss"], r["oc_rs"], me.core_peer())
    near.wait_recv()
    last.wait_recv()
    from_next = rim_r[jnp.where(me.xh == 0, 0, 3)] * has_next
    from_prev = rim_r[jnp.where(me.xh == 0, 3, 0)] * has_prev
    for i in range(4):
        glat[i, 12:16, :] += from_next[4 * i : 4 * i + 4]
        glat[i, 0:4, :] += from_prev[4 * i : 4 * i + 4]
    leave = [pltpu.make_async_copy(glat, gl_o, r["out_sem"].at[0])]
    leave[0].start()
    for k in (Z2, X2, Y2):
        finish_pass(k)
    oc.wait_recv()
    leave.append(pltpu.make_async_copy(obuf, gwo_o, r["out_sem"].at[1]))
    leave[1].start()
    for k in finals:
        arrive(finals[k])
    for xl in range(2):
        for core in range(2):
            dst = gwi_o.at[pl.ds(16 * xl, 16), pl.ds(HALF * core, HALF)]
            leave.append(pltpu.make_async_copy(fin.at[xl, core], dst, r["out_sem"].at[2 + 2 * xl + core]))
            leave[-1].start()
    for copy in leave:
        copy.wait()
    c.drain()


SCRATCH["small_g"] = pltpu.VMEM((16, 32, 128), F32)


def hand_on(loss, gl, gwi, gwo, loss_o, gl_o, gwi_o, gwo_o):
    loss_o[0, 0] = jnp.sum(loss[...]) * (1.0 / POINTS)
    gl_o[...] = gl[...]
    gwi_o[...] = gwi[...]
    for core in range(2):
        for b in range(56):
            vg, hg = b // 8, b % 8
            rows = min(16, VARS - 16 * vg)
            block = gwo[core, b // 16, (b // 4) % 4, b % 4].astype(F32) * (1.0 / SCALE)
            at = core * HALF + 256 * hg
            gwo_o[16 * vg : 16 * vg + rows, at : at + 256] = block[0:rows]


def local(latent, edge_index, edge_weight, noise_seed, noise_table, w_in, w_out, target, area_weight):
    vmem = pl.BlockSpec(memory_space=pltpu.VMEM)
    smem = pl.BlockSpec(memory_space=pltpu.SMEM)
    anywhere = pl.BlockSpec(memory_space=pl.ANY)
    grads = (
        jax.ShapeDtypeStruct((4, 16, LAT), F32),
        jax.ShapeDtypeStruct((32, 2 * HALF), F32),
    )
    blocks = jax.ShapeDtypeStruct((2, 4, 4, 4, 16, 256), BF16)
    made = pl.pallas_call(
        kernel,
        out_shape=(jax.ShapeDtypeStruct((8, 128), F32),) + grads + (blocks,),
        in_specs=[vmem, vmem, vmem, smem] + [vmem] * 5,
        out_specs=(vmem,) + (anywhere,) * 3,
        scratch_shapes=list(SCRATCH.values()),
        compiler_params=pltpu.CompilerParams(
            collective_id=0, has_side_effects=True, vmem_limit_bytes=63 * 2**20
        ),
    )(latent, edge_index, edge_weight, noise_seed, noise_table, w_in, w_out, target, area_weight.reshape(1, -1))
    loss, grad_latent, grad_in, grad_out = pl.pallas_call(
        hand_on,
        out_shape=(jax.ShapeDtypeStruct((1, 1), F32),) + grads + (jax.ShapeDtypeStruct((VARS, 2 * HALF), F32),),
        in_specs=[vmem] * 4,
        out_specs=(smem,) + (vmem,) * 3,
    )(*made)
    return (loss[0, 0], grad_latent, grad_in, grad_out)


def solution(mesh):
    return jax.shard_map(
        local,
        mesh=mesh,
        in_specs=(
            P("member", "space", None),
            P(None, "space"),
            P(None, "space"),
            P("member"),
            P(),
            P("space", None),
            P(),
            P(None, "space"),
            P("space"),
        ),
        out_specs=(P(), P("member", "space", None), P("space", None), P()),
        check_vma=False,
    )
```

```python
import jax
import jax.numpy as jnp
from jax import lax
from jax.experimental import pallas as pl
from jax.experimental.pallas import tpu as pltpu
from jax.sharding import PartitionSpec as P

VARS = 100
HALO = 4
MEMBERS = 16
POINTS = 4096
F32 = jnp.float32
BF16 = jnp.bfloat16
EPS = 1e-05
SMOOTH = 0.04
SCALE = 1024.0
PAIR = 1.0 / (MEMBERS * (MEMBERS - 1))
GELU_C = 0.7978845608028654
MESH = pl.DeviceIdType.MESH

LAT = 1024
HALF = 2048
WIDE = HALF + 256
GROUPS = [
    ("yzx", 0, 384),
    ("zyx", 384, 384),
    ("xzy", 768, 384),
    ("zxy", 1152, 384),
    ("xyz", 1536, 256),
    ("yxz", 1792, 256),
]
SEND_ORDER = (0, 2, 4, 1, 3, 5)
CHUNKS = [(0, (0,)), (768, (2,)), (1536, (4,)), (256, (0, 1)), (512, (1,)), (1024, (2, 3)), (1280, (3,)), (1792, (5,))]
PARTS = [(0, 256), (256, 256), (1536, 512), (512, 512), (1024, 512), (2048, 256)]
ORDERS = ["xyz", "yzx", "zyx", "xzy", "yxz", "zxy"]
X1, Y1, Z2, X2, Y2, OUT = range(6)

DMA = pltpu.SemaphoreType.DMA
SCRATCH = dict(
    wbuf=pltpu.VMEM((4, 4, 4, 16, HALF), BF16),
    wo=pltpu.VMEM((128, HALF), BF16),
    wo_t=pltpu.VMEM((HALF, 128), BF16),
    nbuf=pltpu.VMEM((4, 8, 32, LAT), BF16),
    n_t=pltpu.VMEM((LAT, 1024), BF16),
    xhat=pltpu.VMEM((4, 128, LAT), F32),
    rstd=pltpu.VMEM((4, 128, 128), F32),
    tab=pltpu.VMEM((128, 128), F32),
    small=pltpu.VMEM((3, 128, 128), F32),
    hid=pltpu.VMEM((4, 256, HALF), BF16),
    big=pltpu.VMEM((4, 4, 4, 16, WIDE), F32),
    gpre=pltpu.VMEM((4, 256, HALF), BF16),
    halo_s=pltpu.VMEM((2, 16, LAT), BF16),
    halo_r=pltpu.VMEM((4, 16, LAT), BF16),
    fpart=pltpu.VMEM((4, 8, 32, 128), F32),
    fcore=pltpu.VMEM((2, 8, 32, 128), F32),
    fsum=pltpu.VMEM((2, 8, 32, 128), F32),
    fother=pltpu.VMEM((8, 32, 128), F32),
    gf=pltpu.VMEM((4, 8, 32, 128), BF16),
    gfo=pltpu.VMEM((8, 32, 128), BF16),
    gf_t=pltpu.VMEM((128, 1024), BF16),
    sb1=pltpu.VMEM((4, 4, 4, 16, WIDE), BF16),
    rb1=pltpu.VMEM((2, 4, 4, 16, WIDE), BF16),
    relay=pltpu.VMEM((4, 4, 16, WIDE), BF16),
    q1=pltpu.VMEM((4, 4, 16, WIDE), F32),
    sb2=pltpu.VMEM((4, 4, 16, WIDE), BF16),
    rb2=pltpu.VMEM((3, 4, 16, WIDE), BF16),
    q2=pltpu.VMEM((4, 16, WIDE), F32),
    sb3=pltpu.VMEM((4, 16, WIDE), BF16),
    rb3=pltpu.VMEM((3, 16, WIDE), BF16),
    fin=pltpu.VMEM((2, 2, 16, HALF), F32),
    obuf=pltpu.VMEM((2, 4, 4, 4, 16, 256), BF16),
    gno=pltpu.VMEM((4, 4, 32, LAT), F32),
    gns=pltpu.VMEM((4, 4, 32, LAT), BF16),
    gnr=pltpu.VMEM((4, 4, 32, LAT), BF16),
    rim_s=pltpu.VMEM((2, 16, LAT), F32),
    rim_r=pltpu.VMEM((4, 16, LAT), F32),
    glat=pltpu.VMEM((4, 16, LAT), F32),
    out_sem=DMA((6,)),
    loss_s=pltpu.VMEM((4, 8, 128), F32),
    loss_r=pltpu.VMEM((10, 8, 128), F32),
    ag_ss=DMA((18, 3)),
    ag_rs=DMA((18, 3)),
    rs_ss=DMA((6, 3, 3)),
    rs_rs=DMA((6, 3, 3)),
    ring_ss=DMA((9, 4)),
    ring_rs=DMA((9, 4)),
    oa_ss=DMA((2, 3, 3)),
    oa_rs=DMA((2, 3, 3)),
    fin_ss=DMA((5, 3)),
    fin_rs=DMA((5, 3)),
    n_ss=DMA((4,)),
    n_rs=DMA((4,)),
    gn_ss=DMA((4,)),
    gn_rs=DMA((4,)),
    halo_ss=DMA((3,)),
    halo_rs=DMA((3,)),
    rim_ss=DMA((4,)),
    rim_rs=DMA((4,)),
    f_ss=DMA((2,)),
    f_rs=DMA((2,)),
    g_ss=DMA((3,)),
    g_rs=DMA((3,)),
    oc_ss=DMA,
    oc_rs=DMA,
    l_ss=DMA((10,)),
    l_rs=DMA((10,)),
)


def dot(a, b, dims=((1,), (0,)), precision=None):
    return lax.dot_general(a, b, (dims, ((), ())), precision=precision, preferred_element_type=F32)


class Place:
    def __init__(self):
        m, s = lax.axis_index("member"), lax.axis_index("space")
        self.m, self.s = m, s
        self.xl, self.core = lax.div(m, 2), lax.rem(m, 2)
        self.y, self.z, self.xh = lax.div(s, 8), lax.rem(lax.div(s, 2), 4), lax.rem(s, 2)
        self.x = self.xh * 2 + self.xl
        self.turn = 1 - 2 * self.xh
        self.steps = {(a, 0): getattr(self, a) for a in "yzx"}
        self.peers = {}
        for a in "yzx":
            for k in (1, 2, 3):
                self.steps[a, k] = lax.rem(self.steps[a, 0] + k, 4)
                self.peers[a, k] = self.device(**{b: self.steps[b, k if a == b else 0] for b in "yzx"})

    def device(self, y, z, x):
        return (lax.rem(x, 2) * 2 + self.core, (y * 4 + z) * 2 + lax.div(x, 2))

    def at(self, axis, step=0):
        return self.steps[axis, step]

    def peer(self, axis, step):
        if isinstance(step, int):
            return self.peers[axis, step]
        q = dict(y=self.y, z=self.z, x=self.x)
        q[axis] = lax.rem(q[axis] + step + 4, 4)
        return self.device(**q)

    def core_peer(self):
        return (self.xl * 2 + 1 - self.core, self.s)

    def pair_peer(self):
        return ((1 - self.xl) * 2 + self.core, self.s)


class Copies:
    def __init__(self):
        self.sent = []

    def send(self, src, dst, ss, rs, device):
        copy = pltpu.make_async_remote_copy(
            src_ref=src, dst_ref=dst, send_sem=ss, recv_sem=rs, device_id=device, device_id_type=MESH
        )
        copy.start()
        self.sent.append(copy)
        return copy

    def drain(self):
        for copy in self.sent:
            copy.wait_send()


def arrive(copies):
    for copy in copies:
        copy.wait_recv()


def kernel(lat, eidx, ewt, seed, ntab, w_in, w_out, target, area, loss_o, gl_o, gwi_o, gwo_o, *refs):
    r = dict(zip(SCRATCH, refs))
    wbuf, big, nbuf, n_t, hid, gpre, wo = (r[k] for k in ("wbuf", "big", "nbuf", "n_t", "hid", "gpre", "wo"))
    xhat, rstd, tab, small = r["xhat"], r["rstd"], r["tab"], r["small"]
    me = Place()
    c = Copies()
    col0 = pl.multiple_of(me.core * HALF, 128)

    friends = [me.peer(a, k) for a in "yzx" for k in (1, 2, 3)]
    friends.append(me.core_peer())
    barrier = pltpu.get_barrier_semaphore()
    for d in friends:
        pl.semaphore_signal(barrier, inc=1, device_id=d, device_id_type=MESH)

    wbuf[me.y, me.z, me.x] = w_in[pl.ds(pl.multiple_of(me.xl * 16, 16), 16), pl.ds(col0, HALF)]
    lat32 = [lat[i].astype(F32) for i in range(4)]
    r["halo_s"][0] = jnp.concatenate([v[12:16] for v in lat32], axis=0).astype(BF16)
    r["halo_s"][1] = jnp.concatenate([v[0:4] for v in lat32], axis=0).astype(BF16)
    pl.semaphore_wait(barrier, len(friends))

    halo_s, halo_r = r["halo_s"], r["halo_r"]

    def halo_send(src, dst, k, device):
        return c.send(src, dst, r["halo_ss"].at[k], r["halo_rs"].at[k], device)

    halo = [halo_send(halo_s, halo_r.at[pl.ds(0, 2)], 0, me.peer("x", 2))]

    def gather_send(slot, group, stage, c0, cw):
        order = GROUPS[group][0]
        index = tuple(pl.ds(0, 4) if a in order[:stage] else pl.ds(me.at(a), 1) for a in "yzx")
        index += (slice(None), pl.ds(c0, cw))
        here = wbuf.at[index]
        return [
            c.send(here, here, r["ag_ss"].at[slot, i - 1], r["ag_rs"].at[slot, i - 1], me.peer(order[stage], i))
            for i in (2, 1, 3)
        ]

    gathered = {}

    def gather_stage(stage):
        for g in SEND_ORDER:
            _, c0, cw = GROUPS[g]
            arrive(gathered.pop(g, []))
            gathered[g] = gather_send(6 * stage + g, g, stage, c0, cw)

    gather_stage(0)

    node = lax.broadcasted_iota(jnp.int32, (128, 128), 0)
    row_of = jnp.where(node < 16, node + HALO, jnp.where(node < 20, node - 16, jnp.where(node < 24, node, -1)))
    table_t = jnp.zeros((128, 128), F32)
    for k in range(3):
        table_t = table_t + jnp.where(row_of == eidx[k : k + 1, :], ewt[k : k + 1, :], 0.0)
    tab[...] = table_t
    table = table_t.T[:, :32]
    t_hi = table.astype(BF16)
    t_rest = table - t_hi.astype(F32)
    t_mid = t_rest.astype(BF16)
    t_low = (t_rest - t_mid.astype(F32)).astype(BF16)
    small[0] = jnp.zeros((128, 128), F32)
    small[0, 0:VARS] = target[...]
    small[1] = small[0].T
    small[2] = jnp.broadcast_to(area[...], (128, 128)).T

    arrive(halo)
    halo = [halo_send(halo_r.at[me.xh], halo_r.at[2], 1, me.peer("z", me.turn))]
    gather_stage(1)
    arrive(halo)
    halo = [halo_send(halo_r.at[2], halo_r.at[3], 2, me.peer("y", me.turn))]
    big[0, 0:2, :, :, 0:HALF] = jnp.zeros((2, 4, 16, HALF), F32)
    head = w_out[:, pl.ds(col0, HALF)].astype(F32)
    for v in range(6):
        big[0, v // 4, v % 4, :, 0:HALF] = head[16 * v : 16 * v + 16]
    big[0, 1, 2, 0:4, 0:HALF] = head[96:100]
    wo[...] = big[0, 0:2, :, :, 0:HALF].reshape(128, HALF).astype(BF16)
    r["wo_t"][...] = wo[...].T

    gather_stage(2)

    arrive(halo)
    has_prev = (me.s > 0).astype(F32)
    has_next = (me.s < 31).astype(F32)
    prev_at = jnp.where(me.xh == 0, jnp.where(me.z == 0, 3, 2), 0)
    next_at = jnp.where(me.xh == 1, jnp.where(me.z == 3, 3, 2), 1)
    prev_rows = halo_r[prev_at].astype(F32) * has_prev
    next_rows = halo_r[next_at].astype(F32) * has_next
    normed = []
    for i in range(4):
        edges = [lat[i].astype(F32), prev_rows[4 * i : 4 * i + 4], next_rows[4 * i : 4 * i + 4]]
        window = jnp.concatenate(edges + [jnp.zeros((8, LAT), F32)], axis=0).astype(BF16)
        xhat[i] = dot(t_hi, window) + dot(t_mid, window) + dot(t_low, window)
        scale = 1.0 + ntab[pl.ds(seed[i], 1), :]
        row = me.core * 4 + i

        @pl.loop(0, 4)
        def _(j):
            rows = pl.ds(pl.multiple_of(j * 32, 32), 32)
            a = xhat[i, rows, :]
            centred = a - jnp.mean(a, axis=-1, keepdims=True)
            inv = lax.rsqrt(jnp.mean(centred * centred, axis=-1, keepdims=True) + EPS)
            unit = centred * inv
            xhat[i, rows, :] = unit
            rstd[i, rows, :] = jnp.broadcast_to(inv, (32, 128))
            nbuf[j, row] = (unit * scale).astype(BF16)

        normed.append(c.send(nbuf.at[:, row], nbuf.at[:, row], r["n_ss"].at[i], r["n_rs"].at[i], me.core_peer()))
    arrive(normed)
    for g in range(4):
        n_t[:, 256 * g : 256 * g + 256] = nbuf[g].reshape(256, LAT).T

    fpart, fcore, fsum, fother, gf, gfo = (r[k] for k in ("fpart", "fcore", "fsum", "fother", "gf", "gfo"))
    fpart[...] = jnp.zeros_like(fpart)
    for c0, sources in CHUNKS:
        for g in sources:
            arrive(gathered.pop(g, []))
        cols = slice(c0, c0 + 256)

        w = wbuf[:, :, :, :, cols].reshape(LAT, 256)
        for h in range(4):
            pre = dot(nbuf[h].reshape(256, LAT), w)
            sq = pre * pre
            t = jnp.tanh(pre * (GELU_C + (GELU_C * 0.044715) * sq))
            cdf = 0.5 + 0.5 * t
            act = (pre * cdf).astype(BF16)
            hid[h, :, cols] = act
            slope = cdf + (0.5 * pre) * (1.0 - t * t) * (GELU_C + (3.0 * GELU_C * 0.044715) * sq)
            big[h, :, :, :, cols] = slope.reshape(4, 4, 16, 256)
        for h in range(4):
            fpart[h] += dot(hid[h, :, cols], r["wo_t"][cols, :]).reshape(8, 32, 128)

    f1 = c.send(
        fpart.at[pl.ds(2 * (1 - me.core), 2)], fcore, r["f_ss"].at[0], r["f_rs"].at[0], me.core_peer()
    )
    f1.wait_recv()
    for g in range(2):
        fsum[g] = fpart[2 * me.core + g] + fcore[g]
    f2 = c.send(fsum.at[1 - me.xl], fother, r["f_ss"].at[1], r["f_rs"].at[1], me.pair_peer())
    group = me.core * 2 + me.xl
    f2.wait_recv()

    r["loss_s"][0] = jnp.zeros((8, 128), F32)
    lane = lax.broadcasted_iota(jnp.int32, (8, 128), 1)

    @pl.loop(0, 4)
    def _(j):
        rows = pl.ds(pl.multiple_of(j * 8, 8), 8)
        point = pl.ds(pl.multiple_of(group * 32 + j * 8, 8), 8)
        f = [fsum[me.xl, i, rows, :] for i in range(8)] + [fother[i, rows, :] for i in range(8)]
        weighted = jnp.where(lane < VARS, small[2, point, :] / VARS, 0.0)
        goal = small[1, point, :]
        signs = [jnp.zeros((8, 128), F32) for _ in range(MEMBERS)]
        pairs = jnp.zeros((8, 128), F32)
        for a in range(MEMBERS):
            for b in range(a + 1, MEMBERS):
                d = f[a] - f[b]
                q = d * d + SMOOTH
                inv = lax.rsqrt(q)
                pairs = pairs + q * inv
                sl = d * inv
                signs[a] = signs[a] + sl
                signs[b] = signs[b] - sl
        misfits = jnp.zeros((8, 128), F32)
        for a in range(MEMBERS):
            d = f[a] - goal
            q = d * d + SMOOTH
            inv = lax.rsqrt(q)
            misfits = misfits + q * inv
            grad = (SCALE * weighted) * ((d * inv) * (1.0 / MEMBERS) - PAIR * signs[a])
            r["small_g"][a, rows, :] = grad
        term = misfits * (1.0 / MEMBERS) - PAIR * (pairs + MEMBERS * 0.5 * 0.2)
        r["loss_s"][0] += weighted * term

    for a in range(8):
        gf[group, a] = r["small_g"][a].astype(BF16)
        gfo[a] = r["small_g"][8 + a].astype(BF16)
    gs = [
        c.send(gfo, gf.at[group], r["g_ss"].at[0], r["g_rs"].at[0], me.pair_peer()),
        c.send(gf.at[group], gf.at[group], r["g_ss"].at[1], r["g_rs"].at[1], me.core_peer()),
    ]

    loss_s, loss_r = r["loss_s"], r["loss_r"]
    loss_pending = []

    def loss_send(level):
        if level == 0:
            loss_pending.append(
                [c.send(loss_s.at[0], loss_r.at[0], r["l_ss"].at[0], r["l_rs"].at[0], me.core_peer())]
            )
            return
        axis = "yzx"[level - 1]
        loss_pending.append(
            [
                c.send(
                    loss_s.at[level], loss_r.at[3 * level - 3 + i], r["l_ss"].at[3 * level - 3 + i],
                    r["l_rs"].at[3 * level - 3 + i], me.peer(axis, i),
                )
                for i in (1, 2, 3)
            ]
        )

    def loss_next(level):
        arrive(loss_pending[level])
        if level == 0:
            loss_s[1] = loss_s[0] + loss_r[0]
            return
        v = me.at("yzx"[level - 1])
        base = 3 * level - 3
        own, one, two, three = loss_s[level], loss_r[base + 1], loss_r[base + 2], loss_r[base + 3]
        total = (own + two) + (one + three)
        if level < 3:
            loss_s[level + 1] = total
        else:
            loss_o[...] = total

    loss_send(0)

    def back(h):
        @pl.loop(0, 2)
        def _(j):
            for k in range(4):
                cols = pl.ds(pl.multiple_of(j * 1024 + k * 256, 256), 256)
                slope = big[h, :, :, :, cols].reshape(256, 256)
                gpre[h, :, cols] = (dot(gf[h].reshape(256, 128), wo[:, cols]) * slope).astype(BF16)

    back(group)
    gs[1].wait_recv()
    back((1 - me.core) * 2 + me.xl)
    pair = me.core * 2 + 1 - me.xl
    gs[0].wait_recv()
    gs.append(c.send(gf.at[pair], gf.at[pair], r["g_ss"].at[2], r["g_rs"].at[2], me.core_peer()))
    back(pair)
    gs[2].wait_recv()
    back((1 - me.core) * 2 + 1 - me.xl)
    r["gf_t"][...] = gf[...].reshape(1024, 128).T

    sb1, rb1, q1, sb2, rb2, q2, sb3, rb3, fin, obuf = (
        r[k] for k in ("sb1", "rb1", "q1", "sb2", "rb2", "q2", "sb3", "rb3", "fin", "obuf")
    )
    flight = {}

    def pick(axis, axes, value, cols):
        return tuple(value if a == axis else slice(None) for a in axes) + (slice(None), cols)

    relay = r["relay"]

    def ring_start(k, c0):
        axis = ORDERS[k][0]
        opposite = me.at(axis, 2)
        slot = c0 // 256
        flight[c0] = []
        for i in range(2):
            cols = pl.ds(c0 + 128 * i, 128)
            flight[c0].append(
                c.send(
                    sb1.at[pick(axis, "yzx", opposite, cols)], relay.at[:, :, :, cols],
                    r["ring_ss"].at[slot, i], r["ring_rs"].at[slot, i], me.peer(axis, 1 + 2 * i),
                )
            )

    def ring_pass(k, c0):
        axis = ORDERS[k][0]
        spot = "yzx".index(axis)
        slot = c0 // 256
        passed = []
        for i in range(2):
            flight[c0][i].wait_recv()
            there = me.at(axis, 1 + 2 * i)
            cols = slice(c0 + 128 * i, c0 + 128 * i + 128)
            for v in range(4):
                index = [v, slice(None)]
                index.insert(spot, there)
                index = tuple(index) + (slice(None), cols)
                sb1[index] = (big[index] + relay[v, :, :, cols].astype(F32)).astype(BF16)
            whole = pl.ds(c0, 256)
            passed.append(
                c.send(
                    sb1.at[pick(axis, "yzx", there, whole)], rb1.at[i, :, :, :, whole],
                    r["ring_ss"].at[slot, 2 + i], r["ring_rs"].at[slot, 2 + i], me.peer(axis, 1 + 2 * i),
                )
            )
        flight[(k, 0)] = flight.get((k, 0), []) + passed

    def scatter_send(k, stage):
        c0, cw = PARTS[k]
        cols, order = pl.ds(c0, cw), ORDERS[k]
        axis = order[stage]
        axes = [a for a in "yzx" if a not in order[:stage]]
        src, dst = ((sb2, rb2), (sb3, rb3))[stage - 1]
        flight[(k, stage)] = []
        for i in (2, 1, 3):
            there = me.at(axis, i)
            flight[(k, stage)].append(
                c.send(
                    src.at[pick(axis, axes, there, cols)],
                    dst.at[(i - 1,) + (slice(None),) * (3 - stage) + (cols,)],
                    r["rs_ss"].at[k, stage, i - 1], r["rs_rs"].at[k, stage, i - 1], me.peer(axis, i),
                )
            )

    def scatter_add(k, stage):
        c0, cw = PARTS[k]
        cols, order = slice(c0, c0 + cw), ORDERS[k]
        axis = order[stage]
        axes = [a for a in "yzx" if a not in order[:stage]]
        arrive(flight[(k, stage)])
        own = (big, q1, q2)[stage]
        dst = (rb1, rb2, rb3)[stage]
        where = me.at(axis)
        if stage == 2:
            total = own[where, :, cols]
            for i in range(3):
                total = total + dst[i, :, cols].astype(F32)
            return total
        spot = axes.index(axis)
        keep, send = ((q1, sb2), (q2, sb3))[stage]
        for v in range(4):
            index = [v] + [slice(None)] * (1 - stage)
            index.insert(spot, where)
            total = own[tuple(index) + (slice(None), cols)]
            for i in range(2 + stage):
                total = total + dst[(i, v) + (slice(None),) * (2 - stage) + (cols,)].astype(F32)
            at = (v,) + (slice(None),) * (2 - stage) + (cols,)
            keep[at] = total
            send[at] = total.astype(BF16)

    def advance(k, stage):
        scatter_add(k, stage)
        scatter_send(k, stage + 1)

    finals = {}

    def final_send(k, i, xl, device):
        c0, cw = PARTS[k]
        here = fin.at[xl, me.core, :, pl.ds(c0, cw)]
        return c.send(here, here, r["fin_ss"].at[k, i], r["fin_rs"].at[k, i], device)

    def finish(k):
        c0, cw = PARTS[k]
        fin[me.xl, me.core, :, c0 : c0 + cw] = scatter_add(k, 2) * (1.0 / SCALE)
        finals[k] = [
            final_send(k, 0, me.xl, me.pair_peer()),
            final_send(k, 1, me.xl, me.core_peer()),
        ]

    def finish_pass(k):
        finals[k][0].wait_recv()
        finals[k][0] = final_send(k, 2, 1 - me.xl, me.core_peer())

    out_flight = {}

    def out_stage(part, stage):
        order = ("yzx", "xyz")[part]
        c0 = 128 * part
        if stage == 0:
            if part == 0:
                obuf[me.core, me.y, me.z, me.x] = scatter_add(OUT, 2).astype(BF16)
        else:
            arrive(out_flight[part])
        if stage == 3:
            return
        index = (me.core,)
        index += tuple(pl.ds(0, 4) if a in order[:stage] else pl.ds(me.at(a), 1) for a in "yzx")
        index += (slice(None), pl.ds(c0, 128))
        out_flight[part] = [
            c.send(
                obuf.at[index], obuf.at[index], r["oa_ss"].at[part, stage, i - 1], r["oa_rs"].at[part, stage, i - 1],
                me.peer(order[stage], i),
            )
            for i in (2, 1, 3)
        ]

    @pl.loop(0, 8)
    def _(hg):
        cols = pl.ds(pl.multiple_of(hg * 256, 256), 256)
        part = dot(r["gf_t"][...], hid[:, :, cols].reshape(1024, 256))
        for vg in range(8):
            block = part[16 * vg : 16 * vg + 16]
            y, z, x = vg // 2, (vg % 2) * 2 + hg // 4, hg % 4
            big[y, z, x, :, HALF:WIDE] = block
            sb1[y, z, x, :, HALF:WIDE] = block.astype(BF16)

    ring_start(OUT, HALF)

    def column_part(k, c0):
        cols = slice(c0, c0 + 256)
        for y in range(4):
            rows = slice(256 * y, 256 * y + 256)
            grad = dot(n_t[rows, :], gpre[:, :, cols].reshape(1024, 256)).reshape(4, 4, 16, 256)
            big[y, :, :, :, cols] = grad
            sb1[y, :, :, :, cols] = grad.astype(BF16)
        ring_start(k, c0)

    gno, gns, gnr = r["gno"], r["gns"], r["gnr"]

    def grad_normed(core, dst, n):
        members = pl.ds(pl.multiple_of(core * 128, 128), 128)
        part = dot(gpre[:, members, :].reshape(512, HALF), wbuf[n].reshape(256, HALF), ((1,), (1,)))
        dst[:, :, :, 256 * n : 256 * n + 256] = part.reshape(4, 4, 32, 256).astype(dst.dtype)

    glat, rim_s, rim_r = r["glat"], r["rim_s"], r["rim_r"]

    def norm_back(i):
        scale = 1.0 + ntab[pl.ds(seed[i], 1), :]
        gn[i].wait_recv()
        for j in range(4):
            rows = slice(32 * j, 32 * j + 32)
            g = (gno[j, i] + gnr[j, i].astype(F32)) * scale
            unit = xhat[i, rows, :]
            m1 = jnp.mean(g, axis=-1, keepdims=True)
            m2 = jnp.mean(g * unit, axis=-1, keepdims=True)
            inv = rstd[i, rows, :][:, 0:1]
            xhat[i, rows, :] = inv * (g - m1 - unit * m2)
        rows = dot(tab[0:32, :], xhat[i], precision=lax.Precision.HIGHEST)
        glat[i] = rows[0:16]
        rim_s[0, 4 * i : 4 * i + 4, :] = rows[16:20]
        rim_s[1, 4 * i : 4 * i + 4, :] = rows[20:24]

    def rim_send(src, dst, k, device):
        return c.send(src, dst, r["rim_ss"].at[k], r["rim_rs"].at[k], device)

    column_part(X1, 0)
    column_part(Y1, 256)
    column_part(Z2, 1536)
    column_part(X2, 512)
    column_part(Y2, 1024)
    ring_pass(OUT, HALF)
    column_part(Z2, 1792)
    ring_pass(X1, 0)
    column_part(X2, 768)
    ring_pass(Y1, 256)
    column_part(Y2, 1280)
    ring_pass(Z2, 1536)
    loss_next(0)
    loss_send(1)
    grad_normed(1 - me.core, gns, 0)
    ring_pass(X2, 512)
    grad_normed(1 - me.core, gns, 1)
    ring_pass(Y2, 1024)
    ring_pass(Z2, 1792)
    advance(OUT, 0)
    grad_normed(1 - me.core, gns, 2)
    ring_pass(X2, 768)
    grad_normed(1 - me.core, gns, 3)
    gn = [c.send(gns.at[:, i], gnr.at[:, i], r["gn_ss"].at[i], r["gn_rs"].at[i], me.core_peer()) for i in range(4)]
    ring_pass(Y2, 1280)
    for k in (X1, Y1):
        advance(k, 0)
    loss_next(1)
    loss_send(2)
    for n in range(4):
        grad_normed(me.core, gno, n)
    advance(OUT, 1)
    norm_back(0)
    advance(Z2, 0)
    norm_back(1)
    for k in (X2, Y2):
        advance(k, 0)
    for k in (X1, Y1):
        advance(k, 1)
    out_stage(0, 0)
    out_stage(1, 0)
    loss_next(2)
    loss_send(3)
    norm_back(2)
    norm_back(3)
    near = rim_send(rim_s.at[1 - me.xh], rim_r.at[0], 0, me.peer("x", 2))
    far = rim_send(rim_s.at[me.xh], rim_r.at[1], 1, me.peer("z", -me.turn))
    finish(X1)
    finish(Y1)
    out_stage(0, 1)
    out_stage(1, 1)
    for k in (Z2, X2, Y2):
        advance(k, 1)
    far.wait_recv()
    far = rim_send(rim_r.at[1], rim_r.at[2], 2, me.peer("y", -me.turn))
    for k in (X1, Y1):
        finish_pass(k)
    out_stage(0, 2)
    out_stage(1, 2)
    far.wait_recv()
    carried = jnp.where(me.xh == 0, me.z == 3, me.z == 0)
    last = rim_send(rim_r.at[jnp.where(carried, 2, 1)], rim_r.at[3], 3, me.peer("x", 2))
    for k in (Z2, X2, Y2):
        finish(k)
    loss_next(3)
    out_stage(0, 3)
    out_stage(1, 3)
    own_out = obuf.at[me.core]
    oc = c.send(own_out, own_out, r["oc_ss"], r["oc_rs"], me.core_peer())
    near.wait_recv()
    last.wait_recv()
    from_next = rim_r[jnp.where(me.xh == 0, 0, 3)] * has_next
    from_prev = rim_r[jnp.where(me.xh == 0, 3, 0)] * has_prev
    for i in range(4):
        glat[i, 12:16, :] += from_next[4 * i : 4 * i + 4]
        glat[i, 0:4, :] += from_prev[4 * i : 4 * i + 4]
    leave = [pltpu.make_async_copy(glat, gl_o, r["out_sem"].at[0])]
    leave[0].start()
    for k in (Z2, X2, Y2):
        finish_pass(k)
    oc.wait_recv()
    leave.append(pltpu.make_async_copy(obuf, gwo_o, r["out_sem"].at[1]))
    leave[1].start()
    for k in finals:
        arrive(finals[k])
    for xl in range(2):
        for core in range(2):
            dst = gwi_o.at[pl.ds(16 * xl, 16), pl.ds(HALF * core, HALF)]
            leave.append(pltpu.make_async_copy(fin.at[xl, core], dst, r["out_sem"].at[2 + 2 * xl + core]))
            leave[-1].start()
    for copy in leave:
        copy.wait()
    c.drain()


SCRATCH["small_g"] = pltpu.VMEM((16, 32, 128), F32)


def hand_on(loss, gl, gwi, gwo, loss_o, gl_o, gwi_o, gwo_o):
    loss_o[0, 0] = jnp.sum(loss[...]) * (1.0 / POINTS)
    gl_o[...] = gl[...]
    gwi_o[...] = gwi[...]
    for core in range(2):
        for b in range(56):
            vg, hg = b // 8, b % 8
            rows = min(16, VARS - 16 * vg)
            block = gwo[core, b // 16, (b // 4) % 4, b % 4].astype(F32) * (1.0 / SCALE)
            at = core * HALF + 256 * hg
            gwo_o[16 * vg : 16 * vg + rows, at : at + 256] = block[0:rows]


def local(latent, edge_index, edge_weight, noise_seed, noise_table, w_in, w_out, target, area_weight):
    vmem = pl.BlockSpec(memory_space=pltpu.VMEM)
    smem = pl.BlockSpec(memory_space=pltpu.SMEM)
    anywhere = pl.BlockSpec(memory_space=pl.ANY)
    grads = (
        jax.ShapeDtypeStruct((4, 16, LAT), F32),
        jax.ShapeDtypeStruct((32, 2 * HALF), F32),
    )
    blocks = jax.ShapeDtypeStruct((2, 4, 4, 4, 16, 256), BF16)
    made = pl.pallas_call(
        kernel,
        out_shape=(jax.ShapeDtypeStruct((8, 128), F32),) + grads + (blocks,),
        in_specs=[vmem, vmem, vmem, smem] + [vmem] * 5,
        out_specs=(vmem,) + (anywhere,) * 3,
        scratch_shapes=list(SCRATCH.values()),
        compiler_params=pltpu.CompilerParams(
            collective_id=0, has_side_effects=True, vmem_limit_bytes=63 * 2**20
        ),
    )(latent, edge_index, edge_weight, noise_seed, noise_table, w_in, w_out, target, area_weight.reshape(1, -1))
    loss, grad_latent, grad_in, grad_out = pl.pallas_call(
        hand_on,
        out_shape=(jax.ShapeDtypeStruct((1, 1), F32),) + grads + (jax.ShapeDtypeStruct((VARS, 2 * HALF), F32),),
        in_specs=[vmem] * 4,
        out_specs=(smem,) + (vmem,) * 3,
    )(*made)
    return (loss[0, 0], grad_latent, grad_in, grad_out)


def solution(mesh):
    return jax.shard_map(
        local,
        mesh=mesh,
        in_specs=(
            P("member", "space", None),
            P(None, "space"),
            P(None, "space"),
            P("member"),
            P(),
            P("space", None),
            P(),
            P(None, "space"),
            P("space"),
        ),
        out_specs=(P(), P("member", "space", None), P("space", None), P()),
        check_vma=False,
    )
```
